256 devices in a mesh: dp: 16 (over y, x_lo, core), pencil: 16 (over x_hi, z).
Axes of the slice: x: 4 (x_hi: 2, x_lo: 2; x = x_hi * 2 + x_lo), y: 4, z: 8, core: 2. Of those that a mesh axis runs over, the one named last changes fastest.
Arguments:
- field_in: bfloat16 [16, 32, 512, 2048], P('dp', None, 'pencil'), may hold values from -6 to 6
- cotangent: bfloat16 [16, 32, 512, 2048], P('dp', None, 'pencil'), may hold values from -3 to 3
- spectral_weight: bfloat16 [128, 128, 2048], P('dp', 'pencil'), may hold values from -0.75 to 0.75
Outputs:
- grad_input: bfloat16 [16, 32, 512, 2048], P('dp', None, 'pencil')
- grad_weight: float32 [128, 128, 2048], P('dp', 'pencil')
The draws below stay inside these ranges and needn't reach their ends.
All inputs are finite; a program needn't handle non-finite values.
Results may differ from the reference program's by a relative error of at most 0.025.
Values may be sent and summed in bfloat16 or wider, within the bound.
No kernel may reach another device: no remote copies, remote signals or barrier semaphores. Data moves between devices by JAX's collectives and lax.ppermute only.
A program may use at most 128 MiB of HBM per device.

```python
import math
import jax
import jax.numpy as jnp
from jax import lax

CHANNELS = 32
COLUMNS = 2048
MODES_X = 128
MODES_Y = 128
GRID_ROWS = 512
SAMPLES = 16


def block_scale(key, shape, shards, smallest, high):
    level, own = 1.0, jax.random.fold_in(key, 6)
    for dim, parts in shards:
        draws = jnp.exp(jax.random.uniform(jax.random.fold_in(own, dim), (parts,), jnp.float32, smallest / len(shards), high / len(shards)))
        level = level * jnp.repeat(draws, shape[dim] // parts).reshape([-1 if axis == dim else 1 for axis in range(len(shape))])
    return level


def scatter_about(rng, shape, deviation, bound, shards=(), kind=jnp.bfloat16):
    drawn = deviation * jax.random.normal(rng, shape, jnp.float32)
    if shards:
        drawn = drawn * block_scale(rng, shape, shards, -0.22, 0.18)
    return jnp.clip(drawn, -bound, bound).astype(kind)


def setup_inputs(seed: int = 0) -> dict:
    seeds = jax.random.split(jax.random.key(seed), 4)
    field_in = scatter_about(seeds[0], (SAMPLES, CHANNELS, GRID_ROWS, COLUMNS), 1.0, 6.0, ((0, 16), (2, 16)))
    cotangent = scatter_about(seeds[1], (SAMPLES, CHANNELS, GRID_ROWS, COLUMNS), 0.5, 3.0, ((0, 16), (2, 16)))
    spectral_weight = scatter_about(seeds[2], (MODES_X, MODES_Y, 2 * CHANNELS * CHANNELS), (2 * CHANNELS) ** -0.5, 0.75, ((0, 16), (1, 16)))
    return {"field_in": field_in, "cotangent": cotangent, "spectral_weight": spectral_weight}


def row_matrices(columns, modes):
    frequency = jnp.arange(modes, dtype=jnp.int32)
    position = jnp.arange(columns, dtype=jnp.int32)
    phases = (frequency[:, None] * position[None, :] % columns).astype(jnp.float32) * (2.0 * math.pi / columns)
    paired = jnp.stack([jnp.cos(phases), -jnp.sin(phases)], axis=1)
    forward = (paired / math.sqrt(columns)).reshape(2 * modes, columns).T.astype(jnp.bfloat16)
    factor = jnp.where(frequency == 0, 1.0, 2.0).astype(jnp.float32) / math.sqrt(2 * modes)
    inverse = (paired * factor[:, None, None]).reshape(2 * modes, columns).astype(jnp.bfloat16)
    return (forward, inverse)

def column_matrices(rows, modes):
    counter = jnp.arange(modes, dtype=jnp.int32)
    frequency = jnp.where(counter < modes // 2, counter, rows - modes + counter)
    position = jnp.arange(rows, dtype=jnp.int32)
    phases = (frequency[:, None] * position[None, :] % rows).astype(jnp.float32) * (2.0 * math.pi / rows)
    cosine = jnp.cos(phases)
    sine = jnp.sin(phases)
    forward = jnp.stack([jnp.stack([cosine, sine]), jnp.stack([-sine, cosine])]) / math.sqrt(rows)
    inverse = jnp.stack([jnp.stack([cosine.T, -sine.T]), jnp.stack([sine.T, cosine.T])]) / math.sqrt(modes)
    return (forward.astype(jnp.bfloat16), inverse.astype(jnp.bfloat16))

def column_apply(matrix, values):
    return jnp.einsum('qpjx,scxkp->scjkq', matrix.astype(jnp.float32), values.astype(jnp.float32))

def contract(form, left, right):
    return jnp.einsum(form, left.astype(jnp.float32), right.astype(jnp.float32))

def mix_modes(weights, spectrum):
    weight_real = weights[:, :, :, 0, :]
    weight_imag = weights[:, :, :, 1, :]
    form = 'jkco,scjk->sojk'
    real_part = contract(form, weight_real, spectrum[..., 0]) - contract(form, weight_imag, spectrum[..., 1])
    imag_part = contract(form, weight_real, spectrum[..., 1]) + contract(form, weight_imag, spectrum[..., 0])
    return jnp.stack([real_part, imag_part], axis=-1)

def weight_grad(spectrum, dmixed):
    form = 'scjk,sojk->jkco'
    real_part = contract(form, spectrum[..., 0], dmixed[..., 0]) + contract(form, spectrum[..., 1], dmixed[..., 1])
    imag_part = contract(form, spectrum[..., 0], dmixed[..., 1]) - contract(form, spectrum[..., 1], dmixed[..., 0])
    return jnp.stack([real_part, imag_part], axis=3)

def spectrum_grad(weights, dmixed):
    weight_real = weights[:, :, :, 0, :]
    weight_imag = weights[:, :, :, 1, :]
    form = 'jkco,sojk->scjk'
    real_part = contract(form, weight_real, dmixed[..., 0]) + contract(form, weight_imag, dmixed[..., 1])
    imag_part = contract(form, weight_real, dmixed[..., 1]) - contract(form, weight_imag, dmixed[..., 0])
    return jnp.stack([real_part, imag_part], axis=-1)

def gelu_slope(values):
    normal_cdf = 0.5 * (1.0 + jax.scipy.special.erf(values / math.sqrt(2.0)))
    density = jnp.exp(-0.5 * values * values) / math.sqrt(2.0 * math.pi)
    return normal_cdf + values * density

def reference(field_in, cotangent, spectral_weight):
    row_fwd, row_inv = row_matrices(COLUMNS, MODES_Y)
    col_fwd, col_inv = column_matrices(GRID_ROWS, MODES_X)
    weights = spectral_weight.reshape(MODES_X, MODES_Y, CHANNELS, 2, CHANNELS)

    def one_sample(total, inputs):
        sample = inputs[0][None]
        upstream = inputs[1][None]
        rowspec = jnp.dot(sample.reshape(-1, COLUMNS), row_fwd, preferred_element_type=jnp.float32)
        rowspec = rowspec.astype(jnp.bfloat16).reshape(1, CHANNELS, GRID_ROWS, MODES_Y, 2)
        spectrum = column_apply(col_fwd, rowspec).astype(jnp.bfloat16)
        mixed_modes = mix_modes(weights, spectrum).astype(jnp.bfloat16)
        colback = column_apply(col_inv, mixed_modes).astype(jnp.bfloat16)
        branch = jnp.dot(colback.reshape(-1, 2 * MODES_Y), row_inv, preferred_element_type=jnp.float32)
        pre = sample.astype(jnp.float32) + branch.reshape(1, CHANNELS, GRID_ROWS, COLUMNS)
        dpre = (upstream.astype(jnp.float32) * gelu_slope(pre)).astype(jnp.bfloat16)
        dcolback = jnp.dot(dpre.reshape(-1, COLUMNS), row_inv.T, preferred_element_type=jnp.float32)
        dcolback = dcolback.astype(jnp.bfloat16).reshape(1, CHANNELS, GRID_ROWS, MODES_Y, 2)
        dmixed = column_apply(col_inv.transpose(1, 0, 3, 2), dcolback).astype(jnp.bfloat16)
        total = total + weight_grad(spectrum, dmixed)
        dspectrum = spectrum_grad(weights, dmixed).astype(jnp.bfloat16)
        drowspec = column_apply(col_fwd.transpose(1, 0, 3, 2), dspectrum).astype(jnp.bfloat16)
        back = jnp.dot(drowspec.reshape(-1, 2 * MODES_Y), row_fwd.T, preferred_element_type=jnp.float32)
        result = dpre.astype(jnp.float32) + back.reshape(1, CHANNELS, GRID_ROWS, COLUMNS)
        return (total, result.astype(jnp.bfloat16)[0])
    start = jnp.zeros((MODES_X, MODES_Y, CHANNELS, 2, CHANNELS), jnp.float32)
    total, grads = lax.scan(one_sample, start, (field_in, cotangent))
    return (grads, total.reshape(MODES_X, MODES_Y, 2 * CHANNELS * CHANNELS))
```

```python
import functools
import math

import jax
import jax.numpy as jnp
import ml_dtypes
import numpy as np
from jax import lax
from jax.experimental import pallas as pl
from jax.experimental.pallas import tpu as pltpu
from jax.sharding import PartitionSpec as P

BF16 = jnp.bfloat16
F32 = jnp.float32
LANES = 128
GROUP = 8
SLABS = 16
ROW_TILE = 16
VMEM = 56 * 1024 * 1024


def row_tables(columns, modes):
    k = np.arange(modes, dtype=np.int64)
    y = np.arange(columns, dtype=np.int64)
    phases = (k[:, None] * y[None, :] % columns).astype(np.float32) * np.float32(
        2.0 * math.pi / columns
    )
    paired = np.stack([np.cos(phases), -np.sin(phases)], axis=0)
    forward = (paired / np.float32(math.sqrt(columns))).reshape(2 * modes, columns)
    factor = np.where(k == 0, 1.0, 2.0).astype(np.float32) / np.float32(math.sqrt(2 * modes))
    inverse = (paired * factor[None, :, None]).reshape(2 * modes, columns)
    return forward.astype(ml_dtypes.bfloat16), inverse.astype(ml_dtypes.bfloat16)


def column_tables(rows, modes):
    j = np.arange(modes, dtype=np.int64)
    f = np.where(j < modes // 2, j, rows - modes + j)
    x = np.arange(rows, dtype=np.int64)
    phases = (f[:, None] * x[None, :] % rows).astype(np.float32) * np.float32(2.0 * math.pi / rows)
    c, s = np.cos(phases), np.sin(phases)
    forward = np.block([[c, s], [-s, c]]) / np.float32(math.sqrt(rows))
    inverse = np.block([[c.T, -s.T], [s.T, c.T]]) / np.float32(math.sqrt(modes))
    return forward.astype(ml_dtypes.bfloat16), inverse.astype(ml_dtypes.bfloat16)


def mode_order(channels, parts=2):
    half = channels // 2
    table = np.zeros((parts * channels * GROUP, parts * channels * GROUP), np.float32)
    for c in range(channels):
        for p in range(parts):
            for k in range(GROUP):
                source = ((c // half * parts + p) * half + c % half) * GROUP + k
                table[source, (k * parts + p) * channels + c] = 1.0
    return table.astype(ml_dtypes.bfloat16)


def dot(a, b):
    return jnp.dot(a, b, preferred_element_type=F32)


def dot_t(a, b):
    return lax.dot_general(a, b, (((1,), (1,)), ((), ())), preferred_element_type=F32)


def swap_groups(slabs):
    group = lax.broadcasted_iota(jnp.int32, slabs[0].shape, 1) // GROUP
    bit = 1
    while bit < SLABS:
        low = (group & bit) == 0
        out = list(slabs)
        for i in range(SLABS):
            if i & bit:
                continue
            a, b = slabs[i], slabs[i | bit]
            out[i] = jnp.where(low, a, pltpu.roll(b, bit * GROUP, 1))
            out[i | bit] = jnp.where(low, pltpu.roll(a, LANES - bit * GROUP, 1), b)
        slabs = out
        bit *= 2
    return slabs


def pack(spec, out_ref):
    for p in range(2):
        slabs = [
            spec[c * ROW_TILE : (c + 1) * ROW_TILE, p * LANES : (p + 1) * LANES]
            for c in range(SLABS)
        ]
        for d, slab in enumerate(swap_groups(slabs)):
            out_ref[d, :, p * LANES : (p + 1) * LANES] = slab.astype(BF16)


def unpack(in_ref):
    halves = []
    for p in range(2):
        slabs = [in_ref[d, :, p * LANES : (p + 1) * LANES].astype(F32) for d in range(SLABS)]
        halves.append(jnp.concatenate(swap_groups(slabs), axis=0))
    return jnp.concatenate(halves, axis=1).astype(BF16)


def slope(v):
    a = jnp.abs(v)
    e = jnp.exp(-0.5 * v * v)
    t = 1.0 / (1.0 + (0.3275911 / math.sqrt(2.0)) * a)
    q = 0.5 * 1.061405429 * t - 0.5 * 1.453152027
    q = q * t + 0.5 * 1.421413741
    q = q * t - 0.5 * 0.284496736
    q = q * t + 0.5 * 0.254829592
    g = e * (a * (1.0 / math.sqrt(2.0 * math.pi)) - q * t)
    return jnp.where(v < 0.0, -g, 1.0 + g)


def flat(block):
    return block.reshape(SLABS * ROW_TILE, block.shape[-1])


def row_in_kernel(field_ref, table_ref, out_ref):
    pack(dot(flat(field_ref[...]), table_ref[...]), out_ref)


def middle_kernel(field_ref, cot_ref, back_ref, inv_ref, inv_t_ref, dpre_ref, out_ref):
    back = unpack(back_ref)
    columns = field_ref.shape[-1]
    tile = 512
    total = None
    for start in range(0, columns, tile):
        cut = slice(start, start + tile)
        pre = flat(field_ref[:, :, cut]).astype(F32) + dot(back, inv_ref[:, cut])
        dpre = (flat(cot_ref[:, :, cut]).astype(F32) * slope(pre)).astype(BF16)
        dpre_ref[:, :, cut] = dpre.reshape(SLABS, ROW_TILE, tile)
        term = dot(dpre, inv_t_ref[cut, :])
        total = term if total is None else total + term
    pack(total, out_ref)


def row_out_kernel(dpre_ref, back_ref, table_ref, out_ref):
    back = unpack(back_ref)
    columns = dpre_ref.shape[-1]
    tile = 512
    for start in range(0, columns, tile):
        cut = slice(start, start + tile)
        value = flat(dpre_ref[:, :, cut]).astype(F32) + dot(back, table_ref[:, cut])
        out_ref[:, :, cut] = value.astype(BF16).reshape(SLABS, ROW_TILE, tile)


def stack_parts(values):
    return jnp.concatenate(
        [
            jnp.concatenate(
                [values[:, (2 * h + p) * LANES : (2 * h + p + 1) * LANES] for h in range(2)], axis=1
            )
            for p in range(2)
        ],
        axis=0,
    )


def column_kernel(table_ref, in_ref, out_ref):
    rows = out_ref.shape[0]
    result = dot(table_ref[...], stack_parts(in_ref[...])).astype(BF16)
    for h in range(2):
        for p in range(2):
            at = (2 * h + p) * LANES
            out_ref[:, at : at + LANES] = result[
                p * rows : (p + 1) * rows, h * LANES : (h + 1) * LANES
            ]


def weight_kernel(in_ref, out_ref):
    modes, channels = in_ref.shape[0], in_ref.shape[2]
    zero = jnp.zeros((2 * channels, 2 * channels), F32)
    for j in range(modes):
        for pair in range(GROUP // 2):
            blocks = []
            for i in range(2):
                w = in_ref[j, 2 * pair + i].astype(F32)
                turned = jnp.concatenate([-w[:, channels:], w[:, :channels]], axis=1)
                block = jnp.concatenate([w, turned], axis=0)
                blocks.append(
                    jnp.concatenate([block, zero] if i == 0 else [zero, block], axis=1)
                )
            out_ref[pair, :, j * LANES : (j + 1) * LANES] = jnp.concatenate(blocks, axis=0).astype(
                BF16
            )


def own_row(shape, axis):
    return lax.broadcasted_iota(jnp.int32, shape, axis) % GROUP


def mix_kernel(transposed, in_ref, weight_ref, order_ref, order_t_ref, out_ref):
    values = dot(in_ref[...], order_ref[...]).astype(BF16)
    rows = values.shape[0]
    own = own_row((rows, LANES), 0)
    pieces = []
    for pair in range(GROUP // 2):
        left = values[:, pair * LANES : (pair + 1) * LANES]
        total = jnp.zeros((rows, LANES), F32)
        for j in range(GROUP):
            weight = weight_ref[pair, :, j * LANES : (j + 1) * LANES]
            term = dot_t(left, weight) if transposed else dot(left, weight)
            total = jnp.where(own == j, term, total)
        pieces.append(total.astype(BF16))
    mixed = jnp.concatenate(pieces, axis=1)
    out_ref[...] = dot(mixed, order_t_ref[...]).astype(BF16)


def grad_kernel(spec_ref, dmixed_ref, order_ref, out_ref):
    spec = dot(spec_ref[...], order_ref[...])
    dmixed = dot(dmixed_ref[...], order_ref[...]).astype(BF16)
    rows = spec.shape[0]
    channels = out_ref.shape[2]
    own = own_row((LANES, rows), 1)
    for pair in range(GROUP // 2):
        left = spec[:, pair * LANES : (pair + 1) * LANES].T
        right = dmixed[:, pair * LANES : (pair + 1) * LANES]
        for j in range(GROUP):
            outer = dot(jnp.where(own == j, left, 0.0).astype(BF16), right)
            for i in range(2):
                at = 2 * channels * i
                re = outer[at : at + channels, at : at + 2 * channels]
                im = outer[at + channels : at + 2 * channels, at : at + 2 * channels]
                turned = jnp.concatenate([im[:, channels:], -im[:, :channels]], axis=1)
                out_ref[j, 2 * pair + i] = re + turned


def call(kernel, out, name, **kw):
    return pl.pallas_call(
        kernel,
        out_shape=out,
        name=name,
        compiler_params=pltpu.CompilerParams(vmem_limit_bytes=VMEM),
        **kw,
    )


def shaped(shape, dtype=BF16):
    return jax.ShapeDtypeStruct(shape, dtype)


def rows_call(kernel, name, channels, rows, columns, ins, outs):
    field = pl.BlockSpec((SLABS, ROW_TILE, columns), lambda h, x: (h, x, 0))
    sent = pl.BlockSpec((SLABS, ROW_TILE, 2 * LANES), lambda h, x: (0, x, h))
    specs = {"field": field, "sent": sent}
    shapes = {
        "field": shaped((channels, rows, columns)),
        "sent": shaped((SLABS, rows, 4 * LANES)),
    }

    def spec(kind):
        if kind in specs:
            return specs[kind]
        return pl.BlockSpec(kind, lambda h, x: (0, 0))

    out_shape = [shapes[k] for k in outs]
    out_specs = [specs[k] for k in outs]
    single = len(outs) == 1
    return call(
        kernel,
        out_shape[0] if single else out_shape,
        name,
        grid=(channels // SLABS, rows // ROW_TILE),
        in_specs=[spec(k) for k in ins],
        out_specs=out_specs[0] if single else out_specs,
    )


def across(values, axis):
    return lax.all_to_all(values, axis, split_axis=0, concat_axis=0, tiled=True)


def local(field_in, cotangent, spectral_weight):
    channels, rows_here, columns = field_in.shape[1:]
    pencils = lax.axis_size("pencil")
    modes_y = spectral_weight.shape[1] * pencils
    modes_x = spectral_weight.shape[0] * lax.axis_size("dp")
    height = rows_here * pencils
    wide = 4 * LANES
    row_fwd_t, row_inv = row_tables(columns, modes_y)
    col_fwd, col_inv = column_tables(height, modes_x)
    order = mode_order(channels)
    field = field_in[0]
    cot = cotangent[0]

    def column(table, values, name):
        return call(column_kernel, shaped((table.shape[0] // 2, wide)), name)(
            jnp.asarray(table), values
        )

    def to_pencils(values, name, table):
        return column(table, across(values.reshape(height, wide), "pencil"), name)

    def to_rows(values, name, table):
        return across(column(table, values, name), "pencil").reshape(SLABS, rows_here, wide)

    weights = call(
        weight_kernel, shaped((GROUP // 2, LANES, GROUP * LANES)), "weight_blocks"
    )(spectral_weight.reshape(GROUP, GROUP, channels, 2 * channels))
    order_in, order_out = jnp.asarray(order), jnp.asarray(np.ascontiguousarray(order.T))

    def mix(values, transposed, name):
        return call(
            functools.partial(mix_kernel, transposed), shaped((modes_x, wide)), name
        )(values, weights, order_in, order_out)

    sent = rows_call(
        row_in_kernel, "row_in", channels, rows_here, columns,
        ["field", (columns, 2 * modes_y)], ["sent"],
    )(field, jnp.asarray(np.ascontiguousarray(row_fwd_t.T)))
    spectrum = across(to_pencils(sent, "column_in", col_fwd), "dp")
    mixed = across(mix(spectrum, False, "mix"), "dp")
    back = to_rows(mixed, "column_out", col_inv)
    dpre, sent = rows_call(
        middle_kernel, "middle", channels, rows_here, columns,
        ["field", "field", "sent", (2 * modes_y, columns), (columns, 2 * modes_y)],
        ["field", "sent"],
    )(field, cot, back, jnp.asarray(row_inv), jnp.asarray(np.ascontiguousarray(row_inv.T)))
    dmixed = across(
        to_pencils(sent, "column_in_t", np.ascontiguousarray(col_inv.T)), "dp"
    )
    dspectrum = across(mix(dmixed, True, "mix_t"), "dp")
    back = to_rows(dspectrum, "column_out_t", np.ascontiguousarray(col_fwd.T))
    grad_weight = call(
        grad_kernel, shaped((GROUP, GROUP, channels, 2 * channels), F32), "weight_grad"
    )(spectrum, dmixed, order_in)
    grad_input = rows_call(
        row_out_kernel, "row_out", channels, rows_here, columns,
        ["field", "sent", (2 * modes_y, columns)], ["field"],
    )(dpre, back, jnp.asarray(row_fwd_t))
    return (grad_input[None], grad_weight.reshape(spectral_weight.shape))


def solution(mesh):
    return jax.shard_map(
        local,
        mesh=mesh,
        in_specs=(
            P("dp", None, "pencil", None),
            P("dp", None, "pencil", None),
            P("dp", "pencil", None),
        ),
        out_specs=(P("dp", None, "pencil", None), P("dp", "pencil", None)),
        check_vma=False,
    )
```

```python
import math

import jax
import jax.numpy as jnp
import ml_dtypes
import numpy as np
from jax import lax
from jax.experimental import pallas as pl
from jax.experimental.pallas import tpu as pltpu
from jax.sharding import PartitionSpec as P

BF16 = jnp.bfloat16
F32 = jnp.float32
LANES = 128
GROUP = 8
SLABS = 16
CHUNK = 8
TILE = 256
MIB = 1024 * 1024


def row_tables(columns, modes):
    k = np.arange(modes, dtype=np.int64)
    y = np.arange(columns, dtype=np.int64)
    phases = (k[:, None] * y[None, :] % columns).astype(np.float32) * np.float32(
        2.0 * math.pi / columns
    )
    paired = np.stack([np.cos(phases), -np.sin(phases)], axis=0)
    forward = (paired / np.float32(math.sqrt(columns))).reshape(2 * modes, columns)
    factor = np.where(k == 0, 1.0, 2.0).astype(np.float32) / np.float32(math.sqrt(2 * modes))
    inverse = (paired * factor[None, :, None]).reshape(2 * modes, columns)
    return forward.astype(ml_dtypes.bfloat16), inverse.astype(ml_dtypes.bfloat16)


def column_tables(rows, modes):
    j = np.arange(modes, dtype=np.int64)
    f = np.where(j < modes // 2, j, rows - modes + j)
    x = np.arange(rows, dtype=np.int64)
    phases = (f[:, None] * x[None, :] % rows).astype(np.float32) * np.float32(2.0 * math.pi / rows)
    c, s = np.cos(phases), np.sin(phases)
    forward = np.block([[c, s], [-s, c]]) / np.float32(math.sqrt(rows))
    inverse = np.block([[c.T, -s.T], [s.T, c.T]]) / np.float32(math.sqrt(modes))
    return forward.astype(ml_dtypes.bfloat16), inverse.astype(ml_dtypes.bfloat16)


def mode_order(channels, parts=2):
    half = channels // 2
    table = np.zeros((parts * channels * GROUP, parts * channels * GROUP), np.float32)
    for c in range(channels):
        for p in range(parts):
            for k in range(GROUP):
                source = ((c // half * parts + p) * half + c % half) * GROUP + k
                table[source, (k * parts + p) * channels + c] = 1.0
    return table.astype(ml_dtypes.bfloat16)


def dot(a, b):
    return jnp.dot(a, b, preferred_element_type=F32)


def swap_groups(slabs):
    group = lax.broadcasted_iota(jnp.int32, slabs[0].shape, 1) // GROUP
    bit = 1
    while bit < SLABS:
        low = (group & bit) == 0
        out = list(slabs)
        for i in range(SLABS):
            if i & bit:
                continue
            a, b = slabs[i], slabs[i | bit]
            out[i] = jnp.where(low, a, pltpu.roll(b, bit * GROUP, 1))
            out[i | bit] = jnp.where(low, pltpu.roll(a, LANES - bit * GROUP, 1), b)
        slabs = out
        bit *= 2
    return slabs


def pack(spec, out_ref, half):
    rows = out_ref.shape[1]
    for p in range(2):
        slabs = [
            spec[c * rows : (c + 1) * rows, p * LANES : (p + 1) * LANES] for c in range(SLABS)
        ]
        at = (2 * half + p) * LANES
        for d, slab in enumerate(swap_groups(slabs)):
            out_ref[d, :, at : at + LANES] = slab.astype(BF16)


def unpack(in_ref, half):
    parts = []
    for p in range(2):
        at = (2 * half + p) * LANES
        slabs = [in_ref[d, :, at : at + LANES].astype(F32) for d in range(SLABS)]
        parts.append(jnp.concatenate(swap_groups(slabs), axis=0).astype(BF16))
    return jnp.concatenate(parts, axis=1)


def slope(v):
    e = jnp.exp2((-0.5 / math.log(2.0)) * (v * v)).astype(BF16)
    v = v.astype(BF16)

    def c(value):
        return jnp.asarray(value, BF16)

    a = jnp.abs(v)
    t = c(1.0) / (c(1.0) + c(0.3275911 / math.sqrt(2.0)) * a)
    q = c(0.5 * 1.061405429) * t - c(0.5 * 1.453152027)
    q = q * t + c(0.5 * 1.421413741)
    q = q * t - c(0.5 * 0.284496736)
    q = q * t + c(0.5 * 0.254829592)
    g = e * (a * c(1.0 / math.sqrt(2.0 * math.pi)) - q * t)
    return jnp.where(v < c(0.0), -g, c(1.0) + g)


def flat(block):
    return block.reshape(block.shape[0] * block.shape[1], block.shape[-1])


def load(source, target, sem):
    copy = pltpu.make_async_copy(source, target, sem)
    copy.start()
    return copy


def chunk(i):
    return pl.ds(i * CHUNK, CHUNK)


def row_in_kernel(field_hbm, table_hbm, out_ref, field_ref, table_ref, sems):
    chunks = field_ref.shape[0] // CHUNK
    first = load(table_hbm, table_ref, sems.at[chunks])
    copies = [
        load(field_hbm.at[chunk(i)], field_ref.at[chunk(i)], sems.at[i]) for i in range(chunks)
    ]
    first.wait()
    parts = []
    for i in range(chunks):
        copies[i].wait()
        parts.append(dot(flat(field_ref[i * CHUNK : (i + 1) * CHUNK]), table_ref[...]))
    per_half = SLABS // CHUNK
    for h in range(2):
        pack(jnp.concatenate(parts[h * per_half : (h + 1) * per_half], axis=0), out_ref, h)


def middle_kernel(field_ref, cot_ref, back_ref, inv_ref, inv_t_ref, dpre_ref, out_ref):
    rows, columns = field_ref.shape[1:]
    tall = SLABS * rows
    for h in range(2):
        at = slice(h * SLABS, (h + 1) * SLABS)
        back = unpack(back_ref, h)
        cuts = [slice(start, start + TILE) for start in range(0, columns, TILE)]
        total = jnp.zeros((tall, out_ref.shape[2] // 2), F32)
        branch = dot(back, inv_ref[:, cuts[0]])
        held = None
        for n, cut in enumerate(cuts):
            following = dot(back, inv_ref[:, cuts[n + 1]]) if n + 1 < len(cuts) else None
            pre = flat(field_ref[at, :, cut]).astype(F32) + branch
            dpre = (flat(cot_ref[at, :, cut]) * slope(pre)).astype(BF16)
            if held is not None:
                total = total + dot(held, inv_t_ref[cuts[n - 1], :])
            dpre_ref[at, :, cut] = dpre.reshape(SLABS, rows, TILE)
            held, branch = dpre, following
        total = total + dot(held, inv_t_ref[cuts[-1], :])
        pack(total, out_ref, h)


def row_out_kernel(dpre_ref, back_ref, table_ref, out_hbm, out_ref, sems):
    chunks = dpre_ref.shape[0] // CHUNK
    rows, columns = dpre_ref.shape[1:]
    per_half = SLABS // CHUNK
    stores = []
    for h in range(2):
        back = unpack(back_ref, h)
        for n in range(per_half):
            i = h * per_half + n
            left = back[n * CHUNK * rows : (n + 1) * CHUNK * rows]
            at = slice(i * CHUNK, (i + 1) * CHUNK)
            for start in range(0, columns, TILE):
                cut = slice(start, start + TILE)
                value = flat(dpre_ref[at, :, cut]).astype(F32) + dot(left, table_ref[:, cut])
                out_ref[at, :, cut] = value.astype(BF16).reshape(CHUNK, rows, TILE)
            stores.append(load(out_ref.at[chunk(i)], out_hbm.at[chunk(i)], sems.at[i]))
    for copy in stores:
        copy.wait()


def stack_parts(values):
    return jnp.concatenate(
        [
            jnp.concatenate(
                [values[:, (2 * h + p) * LANES : (2 * h + p + 1) * LANES] for h in range(2)], axis=1
            )
            for p in range(2)
        ],
        axis=0,
    )


def lay_parts(result, out_ref):
    rows = out_ref.shape[0]
    for h in range(2):
        for p in range(2):
            at = (2 * h + p) * LANES
            out_ref[:, at : at + LANES] = result[
                p * rows : (p + 1) * rows, h * LANES : (h + 1) * LANES
            ]


def column_kernel(table_ref, in_ref, out_ref):
    lay_parts(dot(table_ref[...], stack_parts(in_ref[...])).astype(BF16), out_ref)


def turn_kernel(
    table_in_ref, in_ref, order_ref, order_t_ref, table_out_ref, sum_ref, weight_hbm,
    dmixed_ref, out_ref,
    weight_ref, same_ref, cross_ref, grad_ref, spec_ref, sems,
):
    rows = dmixed_ref.shape[0]
    total = weight_ref.shape[0]
    width = weight_ref.shape[1]
    piece = 2 * LANES
    loads = [
        load(weight_hbm.at[pl.ds(at, piece)], weight_ref.at[pl.ds(at, piece)], sems.at[n])
        for n, at in enumerate(range(0, total, piece))
    ]
    lay_parts(dot(table_in_ref[...], stack_parts(in_ref[...])).astype(BF16), dmixed_ref)
    dmixed = dot(dmixed_ref[...], order_ref[...])
    lane = lax.broadcasted_iota(jnp.int32, (rows, LANES), 1)
    low = lane < LANES // 2
    real = lane % (LANES // 2) < LANES // 4
    for pair in range(GROUP // 2):
        both = dmixed[:, pair * LANES : (pair + 1) * LANES]
        other = pltpu.roll(both, LANES // 2, 1)
        for i in range(2):
            same = jnp.where(low, both, other) if i == 0 else jnp.where(low, other, both)
            turned = pltpu.roll(same, LANES // 4, 1)
            at = pl.ds(2 * pair + i, rows, stride=GROUP)
            same_ref[at, :] = same
            cross_ref[at, :] = jnp.where(real, turned, -turned)
    for n, at in enumerate(range(0, total, piece)):
        loads[n].wait()
        cut = slice(at, at + piece)
        weight = weight_ref[cut, :]
        copies = width // LANES
        same = jnp.concatenate([same_ref[cut, :].astype(BF16)] * copies, axis=1)
        cross = jnp.concatenate([cross_ref[cut, :].astype(BF16)] * copies, axis=1)
        re = dot(weight * same, sum_ref[...])
        im = dot(weight * cross, sum_ref[...])
        grad_ref[cut, :] = re + pltpu.roll(im, LANES // 4, 1)
    for pair in range(GROUP // 2):
        first = grad_ref[pl.ds(2 * pair, rows, stride=GROUP), :]
        second = grad_ref[pl.ds(2 * pair + 1, rows, stride=GROUP), :]
        both = jnp.where(low, first, pltpu.roll(second, LANES // 2, 1))
        spec_ref[:, pair * LANES : (pair + 1) * LANES] = both.astype(BF16)
    dspec = dot(spec_ref[...], order_t_ref[...]).astype(BF16)
    lay_parts(dot(table_out_ref[...], stack_parts(dspec)).astype(BF16), out_ref)


def weight_kernel(in_ref, out_ref):
    modes, channels = in_ref.shape[0], in_ref.shape[2]
    zero = jnp.zeros((2 * channels, 2 * channels), F32)
    for j in range(modes):
        for pair in range(GROUP // 2):
            blocks = []
            for i in range(2):
                w = in_ref[j, 2 * pair + i].astype(F32)
                turned = jnp.concatenate([-w[:, channels:], w[:, :channels]], axis=1)
                block = jnp.concatenate([w, turned], axis=0)
                blocks.append(
                    jnp.concatenate([block, zero] if i == 0 else [zero, block], axis=1)
                )
            out_ref[pair, :, j * LANES : (j + 1) * LANES] = jnp.concatenate(blocks, axis=0).astype(
                BF16
            )


def own_row(shape, axis):
    return lax.broadcasted_iota(jnp.int32, shape, axis) % GROUP


def mix_kernel(in_ref, weight_ref, order_ref, order_t_ref, out_ref):
    values = dot(in_ref[...], order_ref[...]).astype(BF16)
    rows = values.shape[0]
    own = own_row((rows, LANES), 0)
    pieces = []
    for pair in range(GROUP // 2):
        left = values[:, pair * LANES : (pair + 1) * LANES]
        total = jnp.zeros((rows, LANES), F32)
        for j in range(GROUP):
            weight = weight_ref[pair, :, j * LANES : (j + 1) * LANES]
            term = dot(left, weight)
            total = jnp.where(own == j, term, total)
        pieces.append(total.astype(BF16))
    mixed = jnp.concatenate(pieces, axis=1)
    out_ref[...] = dot(mixed, order_t_ref[...]).astype(BF16)


def grad_kernel(spec_ref, dmixed_ref, order_ref, out_ref):
    spec = dot(spec_ref[...], order_ref[...])
    dmixed = dot(dmixed_ref[...], order_ref[...]).astype(BF16)
    rows = spec.shape[0]
    channels = out_ref.shape[2]
    own = own_row((LANES, rows), 1)
    for pair in range(GROUP // 2):
        left = spec[:, pair * LANES : (pair + 1) * LANES].T
        right = dmixed[:, pair * LANES : (pair + 1) * LANES]
        for j in range(GROUP):
            outer = dot(jnp.where(own == j, left, 0.0).astype(BF16), right)
            for i in range(2):
                at = 2 * channels * i
                re = outer[at : at + channels, at : at + 2 * channels]
                im = outer[at + channels : at + 2 * channels, at : at + 2 * channels]
                turned = jnp.concatenate([im[:, channels:], -im[:, :channels]], axis=1)
                out_ref[j, 2 * pair + i] = re + turned


def shaped(shape, dtype=BF16):
    return jax.ShapeDtypeStruct(shape, dtype)


def call(kernel, out, name, vmem=16, **kw):
    return pl.pallas_call(
        kernel,
        out_shape=out,
        name=name,
        compiler_params=pltpu.CompilerParams(vmem_limit_bytes=vmem * MIB),
        **kw,
    )


ANY = pl.BlockSpec(memory_space=pl.ANY)
WHOLE = pl.BlockSpec(memory_space=pltpu.VMEM)


def buffers(*shapes):
    return [pltpu.VMEM(shape, BF16) for shape in shapes]


def sems(count):
    return pltpu.SemaphoreType.DMA((count,))


def across(values, axis):
    return lax.all_to_all(values, axis, split_axis=0, concat_axis=0, tiled=True)


def local(field_in, cotangent, spectral_weight):
    channels, rows_here, columns = field_in.shape[1:]
    pencils = lax.axis_size("pencil")
    modes_y = spectral_weight.shape[1] * pencils
    modes_x = spectral_weight.shape[0] * lax.axis_size("dp")
    height = rows_here * pencils
    wide = 4 * LANES
    chunks = channels // CHUNK
    row_fwd_t, row_inv = row_tables(columns, modes_y)
    col_fwd, col_inv = column_tables(height, modes_x)
    order = mode_order(channels)
    lane = np.arange(spectral_weight.shape[2])
    summed = (lane[:, None] // (2 * channels) == np.arange(LANES)[None, :]).astype(
        ml_dtypes.bfloat16
    )
    field = field_in[0]
    cot = cotangent[0]
    field_shape = field.shape
    sent_shape = (SLABS, rows_here, wide)
    tall = (columns, 2 * modes_y)

    def turned(table):
        return jnp.asarray(np.ascontiguousarray(table.T))

    def column(table, values, name):
        return call(column_kernel, shaped((table.shape[0] // 2, wide)), name)(table, values)

    gathered = lax.all_gather(spectral_weight, "dp", axis=0, tiled=True)
    weights = call(
        weight_kernel, shaped((GROUP // 2, LANES, GROUP * LANES)), "weight_blocks"
    )(spectral_weight.reshape(GROUP, GROUP, channels, 2 * channels))
    order_in, order_out = jnp.asarray(order), turned(order)

    sent = call(
        row_in_kernel, shaped(sent_shape), "row_in", 60,
        in_specs=[ANY] * 2, out_specs=WHOLE,
        scratch_shapes=buffers(field_shape, tall) + [sems(chunks + 1)],
    )(field, turned(row_fwd_t))
    arrived = across(sent, "pencil").reshape(height, wide)
    spectrum = across(column(jnp.asarray(col_fwd), arrived, "column_in"), "dp")
    mixed = across(
        call(mix_kernel, shaped((modes_x, wide)), "mix")(spectrum, weights, order_in, order_out),
        "dp",
    )
    back = across(column(jnp.asarray(col_inv), mixed, "column_out"), "pencil")
    dpre, sent = call(
        middle_kernel, [shaped(field_shape), shaped(sent_shape)], "middle", 16,
        in_specs=[WHOLE] * 5, out_specs=[WHOLE] * 2,
    )(field, cot, back.reshape(sent_shape), jnp.asarray(row_inv), turned(row_inv))
    arrived = across(sent, "pencil").reshape(height, wide)
    modes = modes_x * GROUP
    dmixed, sent = call(
        turn_kernel, [shaped((modes_x, wide)), shaped((height, wide))], "turn", 28,
        in_specs=[WHOLE] * 6 + [ANY], out_specs=[WHOLE] * 2,
        scratch_shapes=[
            pltpu.VMEM((modes, spectral_weight.shape[2]), BF16),
            pltpu.VMEM((modes, LANES), F32),
            pltpu.VMEM((modes, LANES), F32),
            pltpu.VMEM((modes, LANES), F32),
            pltpu.VMEM((modes_x, wide), BF16),
            sems(modes // (2 * LANES)),
        ],
    )(
        turned(col_inv), arrived, order_in, order_out, turned(col_fwd), jnp.asarray(summed),
        gathered.reshape(modes, spectral_weight.shape[2]),
    )
    back = across(sent, "pencil").reshape(sent_shape)
    grad_weight = call(
        grad_kernel, shaped((GROUP, GROUP, channels, 2 * channels), F32), "weight_grad"
    )(spectrum, across(dmixed, "dp"), order_in)
    grad_input = call(
        row_out_kernel, shaped(field_shape), "row_out", 16,
        in_specs=[WHOLE] * 3, out_specs=ANY,
        scratch_shapes=buffers(field_shape) + [sems(chunks)],
    )(dpre, back, jnp.asarray(row_fwd_t))
    return (grad_input[None], grad_weight.reshape(spectral_weight.shape))


def solution(mesh):
    return jax.shard_map(
        local,
        mesh=mesh,
        in_specs=(
            P("dp", None, "pencil", None),
            P("dp", None, "pencil", None),
            P("dp", "pencil", None),
        ),
        out_specs=(P("dp", None, "pencil", None), P("dp", "pencil", None)),
        check_vma=False,
    )
```

```python
import math

import jax
import jax.numpy as jnp
import ml_dtypes
import numpy as np
from jax import lax
from jax.experimental import pallas as pl
from jax.experimental.pallas import tpu as pltpu
from jax.sharding import PartitionSpec as P

BF16 = jnp.bfloat16
F32 = jnp.float32
LANES = 128
GROUP = 8
SLABS = 16
CHUNK = 8
TILE = 256
SPANS = 2
MIB = 1024 * 1024


def row_tables(columns, modes):
    k = np.arange(modes, dtype=np.int64)
    y = np.arange(columns, dtype=np.int64)
    phases = (k[:, None] * y[None, :] % columns).astype(np.float32) * np.float32(
        2.0 * math.pi / columns
    )
    paired = np.stack([np.cos(phases), -np.sin(phases)], axis=0)
    forward = (paired / np.float32(math.sqrt(columns))).reshape(2 * modes, columns)
    factor = np.where(k == 0, 1.0, 2.0).astype(np.float32) / np.float32(math.sqrt(2 * modes))
    inverse = (paired * factor[None, :, None]).reshape(2 * modes, columns)
    return forward.astype(ml_dtypes.bfloat16), inverse.astype(ml_dtypes.bfloat16)


def column_tables(rows, modes):
    j = np.arange(modes, dtype=np.int64)
    f = np.where(j < modes // 2, j, rows - modes + j)
    x = np.arange(rows, dtype=np.int64)
    phases = (f[:, None] * x[None, :] % rows).astype(np.float32) * np.float32(2.0 * math.pi / rows)
    c, s = np.cos(phases), np.sin(phases)
    forward = np.block([[c, s], [-s, c]]) / np.float32(math.sqrt(rows))
    inverse = np.block([[c.T, -s.T], [s.T, c.T]]) / np.float32(math.sqrt(modes))
    return forward.astype(ml_dtypes.bfloat16), inverse.astype(ml_dtypes.bfloat16)


def mode_order(channels, parts=2):
    half = channels // 2
    table = np.zeros((parts * channels * GROUP, parts * channels * GROUP), np.float32)
    for c in range(channels):
        for p in range(parts):
            for k in range(GROUP):
                source = ((c // half * parts + p) * half + c % half) * GROUP + k
                table[source, (k * parts + p) * channels + c] = 1.0
    return table.astype(ml_dtypes.bfloat16)


def dot(a, b):
    return jnp.dot(a, b, preferred_element_type=F32)


def swap_groups(slabs):
    group = lax.broadcasted_iota(jnp.int32, slabs[0].shape, 1) // GROUP
    bit = 1
    while bit < SLABS:
        low = (group & bit) == 0
        out = list(slabs)
        for i in range(SLABS):
            if i & bit:
                continue
            a, b = slabs[i], slabs[i | bit]
            out[i] = jnp.where(low, a, pltpu.roll(b, bit * GROUP, 1))
            out[i | bit] = jnp.where(low, pltpu.roll(a, LANES - bit * GROUP, 1), b)
        slabs = out
        bit *= 2
    return slabs


def pack(spec, out_ref, half):
    rows = out_ref.shape[1]
    for p in range(2):
        slabs = [
            spec[c * rows : (c + 1) * rows, p * LANES : (p + 1) * LANES] for c in range(SLABS)
        ]
        at = (2 * half + p) * LANES
        for d, slab in enumerate(swap_groups(slabs)):
            out_ref[d, :, at : at + LANES] = slab.astype(BF16)


def unpack(in_ref, half):
    parts = []
    for p in range(2):
        at = (2 * half + p) * LANES
        slabs = [in_ref[d, :, at : at + LANES].astype(F32) for d in range(SLABS)]
        parts.append(jnp.concatenate(swap_groups(slabs), axis=0).astype(BF16))
    return jnp.concatenate(parts, axis=1)


def slope(v):
    e = jnp.exp2((-0.5 / math.log(2.0)) * (v * v)).astype(BF16)
    v = v.astype(BF16)

    def c(value):
        return jnp.asarray(value, BF16)

    a = jnp.abs(v)
    t = c(1.0) / (c(1.0) + c(0.3275911 / math.sqrt(2.0)) * a)
    q = c(0.5 * 1.061405429) * t - c(0.5 * 1.453152027)
    q = q * t + c(0.5 * 1.421413741)
    q = q * t - c(0.5 * 0.284496736)
    q = q * t + c(0.5 * 0.254829592)
    g = e * (a * c(1.0 / math.sqrt(2.0 * math.pi)) - q * t)
    return jnp.where(v < c(0.0), -g, c(1.0) + g)


def flat(block):
    return block.reshape(block.shape[0] * block.shape[1], block.shape[-1])


def load(source, target, sem):
    copy = pltpu.make_async_copy(source, target, sem)
    copy.start()
    return copy


def chunk(i):
    return pl.ds(i * CHUNK, CHUNK)


def row_in_kernel(
    field_hbm, table_hbm, weight_hbm, out_ref, passed_hbm, field_ref, table_ref, sems
):
    chunks = field_ref.shape[0] // CHUNK
    first = load(table_hbm, table_ref, sems.at[chunks])
    copies = [
        load(field_hbm.at[chunk(i)], field_ref.at[chunk(i)], sems.at[i]) for i in range(chunks)
    ]
    passed = load(weight_hbm, passed_hbm, sems.at[chunks + 1])
    first.wait()
    parts = []
    for i in range(chunks):
        copies[i].wait()
        parts.append(dot(flat(field_ref[i * CHUNK : (i + 1) * CHUNK]), table_ref[...]))
    per_half = SLABS // CHUNK
    for h in range(2):
        pack(jnp.concatenate(parts[h * per_half : (h + 1) * per_half], axis=0), out_ref, h)
    passed.wait()


def middle_kernel(
    field_hbm, cot_hbm, back_ref, inv_hbm, inv_t_hbm, dpre_hbm, out_ref,
    field_ref, cot_ref, inv_ref, inv_t_ref, dpre_ref, sems, sent_sems,
):
    rows, columns = field_ref.shape[1:]
    span = columns // SPANS
    inv_load = load(inv_hbm, inv_ref, sems.at[0])
    inv_t_load = None
    loads = []
    for h in range(2):
        for n in range(SPANS):
            at = (pl.ds(h * SLABS, SLABS), slice(None), pl.ds(n * span, span))
            slot = 2 + 2 * (h * SPANS + n)
            loads.append(
                (
                    load(field_hbm.at[at], field_ref.at[at], sems.at[slot]),
                    load(cot_hbm.at[at], cot_ref.at[at], sems.at[slot + 1]),
                )
            )
            if inv_t_load is None:
                inv_t_load = load(inv_t_hbm, inv_t_ref, sems.at[1])
    tall = SLABS * rows
    stores = []
    for h in range(2):
        at = slice(h * SLABS, (h + 1) * SLABS)
        back = unpack(back_ref, h)
        total = jnp.zeros((tall, out_ref.shape[2] // 2), F32)
        if h == 0:
            inv_load.wait()
        for n in range(SPANS):
            for copy in loads[h * SPANS + n]:
                copy.wait()
            if h == 0 and n == 0:
                inv_t_load.wait()
            cuts = [slice(y, y + TILE) for y in range(n * span, (n + 1) * span, TILE)]
            branch = dot(back, inv_ref[:, cuts[0]])
            held = None
            for m, cut in enumerate(cuts):
                following = dot(back, inv_ref[:, cuts[m + 1]]) if m + 1 < len(cuts) else None
                pre = flat(field_ref[at, :, cut]).astype(F32) + branch
                dpre = (flat(cot_ref[at, :, cut]) * slope(pre)).astype(BF16)
                if held is not None:
                    total = total + dot(held, inv_t_ref[cuts[m - 1], :])
                dpre_ref[at, :, cut] = dpre.reshape(SLABS, rows, TILE)
                held, branch = dpre, following
            total = total + dot(held, inv_t_ref[cuts[-1], :])
            place = (pl.ds(h * SLABS, SLABS), slice(None), pl.ds(n * span, span))
            stores.append(
                load(dpre_ref.at[place], dpre_hbm.at[place], sent_sems.at[h * SPANS + n])
            )
        pack(total, out_ref, h)
    for copy in stores:
        copy.wait()


def row_out_kernel(
    dpre_hbm, back_ref, table_hbm, out_hbm, dpre_ref, table_ref, out_ref, sems, sent_sems
):
    chunks = dpre_ref.shape[0] // CHUNK
    rows, columns = dpre_ref.shape[1:]
    per_half = SLABS // CHUNK
    table_load = load(table_hbm, table_ref, sems.at[chunks])
    loads = [
        load(dpre_hbm.at[chunk(i)], dpre_ref.at[chunk(i)], sems.at[i]) for i in range(chunks)
    ]
    stores = []
    for h in range(2):
        back = unpack(back_ref, h)
        if h == 0:
            table_load.wait()
        for n in range(per_half):
            i = h * per_half + n
            loads[i].wait()
            left = back[n * CHUNK * rows : (n + 1) * CHUNK * rows]
            at = slice(i * CHUNK, (i + 1) * CHUNK)
            for start in range(0, columns, TILE):
                cut = slice(start, start + TILE)
                value = flat(dpre_ref[at, :, cut]).astype(F32) + dot(left, table_ref[:, cut])
                out_ref[at, :, cut] = value.astype(BF16).reshape(CHUNK, rows, TILE)
            stores.append(load(out_ref.at[chunk(i)], out_hbm.at[chunk(i)], sent_sems.at[i]))
    for copy in stores:
        copy.wait()


def stack_parts(values):
    return jnp.concatenate(
        [
            jnp.concatenate(
                [values[:, (2 * h + p) * LANES : (2 * h + p + 1) * LANES] for h in range(2)], axis=1
            )
            for p in range(2)
        ],
        axis=0,
    )


def lay_parts(result, out_ref):
    rows = out_ref.shape[0]
    for h in range(2):
        for p in range(2):
            at = (2 * h + p) * LANES
            out_ref[:, at : at + LANES] = result[
                p * rows : (p + 1) * rows, h * LANES : (h + 1) * LANES
            ]


def column_kernel(table_ref, in_ref, out_ref):
    lay_parts(dot(table_ref[...], stack_parts(in_ref[...])).astype(BF16), out_ref)


def turn_kernel(
    dmixed_ref, order_ref, order_t_ref, table_out_ref, sum_ref, weight_hbm, out_ref,
    weight_ref, same_ref, cross_ref, grad_ref, spec_ref, sems,
):
    rows = dmixed_ref.shape[0]
    total = weight_ref.shape[0]
    width = weight_ref.shape[1]
    piece = 2 * LANES
    loads = [
        load(weight_hbm.at[pl.ds(at, piece)], weight_ref.at[pl.ds(at, piece)], sems.at[n])
        for n, at in enumerate(range(0, total, piece))
    ]
    dmixed = dot(dmixed_ref[...], order_ref[...])
    lane = lax.broadcasted_iota(jnp.int32, (rows, LANES), 1)
    low = lane < LANES // 2
    real = lane % (LANES // 2) < LANES // 4
    for pair in range(GROUP // 2):
        both = dmixed[:, pair * LANES : (pair + 1) * LANES]
        other = pltpu.roll(both, LANES // 2, 1)
        for i in range(2):
            same = jnp.where(low, both, other) if i == 0 else jnp.where(low, other, both)
            turned = pltpu.roll(same, LANES // 4, 1)
            at = pl.ds(2 * pair + i, rows, stride=GROUP)
            same_ref[at, :] = same
            cross_ref[at, :] = jnp.where(real, turned, -turned)
    for n, at in enumerate(range(0, total, piece)):
        loads[n].wait()
        cut = slice(at, at + piece)
        weight = weight_ref[cut, :]
        copies = width // LANES
        same = jnp.concatenate([same_ref[cut, :].astype(BF16)] * copies, axis=1)
        cross = jnp.concatenate([cross_ref[cut, :].astype(BF16)] * copies, axis=1)
        re = dot(weight * same, sum_ref[...])
        im = dot(weight * cross, sum_ref[...])
        grad_ref[cut, :] = re + pltpu.roll(im, LANES // 4, 1)
    for pair in range(GROUP // 2):
        first = grad_ref[pl.ds(2 * pair, rows, stride=GROUP), :]
        second = grad_ref[pl.ds(2 * pair + 1, rows, stride=GROUP), :]
        both = jnp.where(low, first, pltpu.roll(second, LANES // 2, 1))
        spec_ref[:, pair * LANES : (pair + 1) * LANES] = both.astype(BF16)
    dspec = dot(spec_ref[...], order_t_ref[...]).astype(BF16)
    lay_parts(dot(table_out_ref[...], stack_parts(dspec)).astype(BF16), out_ref)


def weight_kernel(in_ref, out_ref):
    modes, channels = in_ref.shape[0], in_ref.shape[2]
    zero = jnp.zeros((2 * channels, 2 * channels), F32)
    for j in range(modes):
        for pair in range(GROUP // 2):
            blocks = []
            for i in range(2):
                w = in_ref[j, 2 * pair + i].astype(F32)
                turned = jnp.concatenate([-w[:, channels:], w[:, :channels]], axis=1)
                block = jnp.concatenate([w, turned], axis=0)
                blocks.append(
                    jnp.concatenate([block, zero] if i == 0 else [zero, block], axis=1)
                )
            out_ref[pair, :, j * LANES : (j + 1) * LANES] = jnp.concatenate(blocks, axis=0).astype(
                BF16
            )


def own_row(shape, axis):
    return lax.broadcasted_iota(jnp.int32, shape, axis) % GROUP


def mix_kernel(in_ref, weight_ref, order_ref, order_t_ref, out_ref):
    values = dot(in_ref[...], order_ref[...]).astype(BF16)
    rows = values.shape[0]
    own = own_row((rows, LANES), 0)
    pieces = []
    for pair in range(GROUP // 2):
        left = values[:, pair * LANES : (pair + 1) * LANES]
        total = jnp.zeros((rows, LANES), F32)
        for j in range(GROUP):
            weight = weight_ref[pair, :, j * LANES : (j + 1) * LANES]
            term = dot(left, weight)
            total = jnp.where(own == j, term, total)
        pieces.append(total.astype(BF16))
    mixed = jnp.concatenate(pieces, axis=1)
    out_ref[...] = dot(mixed, order_t_ref[...]).astype(BF16)


def grad_kernel(spec_ref, dmixed_ref, order_ref, after_hbm, out_ref):
    spec = dot(spec_ref[...], order_ref[...])
    dmixed = dot(dmixed_ref[...], order_ref[...]).astype(BF16)
    rows = spec.shape[0]
    channels = out_ref.shape[2]
    own = own_row((LANES, rows), 1)
    for pair in range(GROUP // 2):
        left = spec[:, pair * LANES : (pair + 1) * LANES].T
        right = dmixed[:, pair * LANES : (pair + 1) * LANES]
        for j in range(GROUP):
            outer = dot(jnp.where(own == j, left, 0.0).astype(BF16), right)
            for i in range(2):
                at = 2 * channels * i
                re = outer[at : at + channels, at : at + 2 * channels]
                im = outer[at + channels : at + 2 * channels, at : at + 2 * channels]
                turned = jnp.concatenate([im[:, channels:], -im[:, :channels]], axis=1)
                out_ref[j, 2 * pair + i] = re + turned


def shaped(shape, dtype=BF16):
    return jax.ShapeDtypeStruct(shape, dtype)


def call(kernel, out, name, vmem=16, **kw):
    return pl.pallas_call(
        kernel,
        out_shape=out,
        name=name,
        compiler_params=pltpu.CompilerParams(vmem_limit_bytes=vmem * MIB),
        **kw,
    )


HBM = pl.BlockSpec(memory_space=pltpu.HBM)
WHOLE = pl.BlockSpec(memory_space=pltpu.VMEM)


def buffers(*shapes):
    return [pltpu.VMEM(shape, BF16) for shape in shapes]


def sems(count):
    return pltpu.SemaphoreType.DMA((count,))


def across(values, axis):
    return lax.all_to_all(values, axis, split_axis=0, concat_axis=0, tiled=True)


def local(field_in, cotangent, spectral_weight):
    channels, rows_here, columns = field_in.shape[1:]
    pencils = lax.axis_size("pencil")
    modes_y = spectral_weight.shape[1] * pencils
    modes_x = spectral_weight.shape[0] * lax.axis_size("dp")
    height = rows_here * pencils
    wide = 4 * LANES
    chunks = channels // CHUNK
    row_fwd_t, row_inv = row_tables(columns, modes_y)
    col_fwd, col_inv = column_tables(height, modes_x)
    order = mode_order(channels)
    lane = np.arange(spectral_weight.shape[2])
    summed = (lane[:, None] // (2 * channels) == np.arange(LANES)[None, :]).astype(
        ml_dtypes.bfloat16
    )
    field = field_in[0]
    cot = cotangent[0]
    field_shape = field.shape
    sent_shape = (SLABS, rows_here, wide)
    narrow, tall = (2 * modes_y, columns), (columns, 2 * modes_y)

    def turned(table):
        return jnp.asarray(np.ascontiguousarray(table.T))

    def column(table, values, name):
        return call(column_kernel, shaped((table.shape[0] // 2, wide)), name)(table, values)

    weights = call(
        weight_kernel, shaped((GROUP // 2, LANES, GROUP * LANES)), "weight_blocks"
    )(spectral_weight.reshape(GROUP, GROUP, channels, 2 * channels))
    order_in, order_out = jnp.asarray(order), turned(order)

    sent, passed = call(
        row_in_kernel, [shaped(sent_shape), shaped(spectral_weight.shape)], "row_in", 60,
        in_specs=[HBM] * 3, out_specs=[WHOLE, HBM],
        scratch_shapes=buffers(field_shape, tall) + [sems(chunks + 2)],
    )(field, turned(row_fwd_t), spectral_weight)
    gathered = lax.all_gather(passed, "dp", axis=0, tiled=True)
    arrived = across(sent, "pencil").reshape(height, wide)
    spectrum = across(column(jnp.asarray(col_fwd), arrived, "column_in"), "dp")
    mixed = across(
        call(mix_kernel, shaped((modes_x, wide)), "mix")(spectrum, weights, order_in, order_out),
        "dp",
    )
    back = across(column(jnp.asarray(col_inv), mixed, "column_out"), "pencil")
    dpre, sent = call(
        middle_kernel, [shaped(field_shape), shaped(sent_shape)], "middle", 60,
        in_specs=[HBM, HBM, WHOLE, HBM, HBM], out_specs=[HBM, WHOLE],
        scratch_shapes=buffers(field_shape, field_shape, narrow, tall, field_shape)
        + [sems(2 + 4 * SPANS), sems(2 * SPANS)],
    )(field, cot, back.reshape(sent_shape), jnp.asarray(row_inv), turned(row_inv))
    arrived = across(sent, "pencil").reshape(height, wide)
    modes = modes_x * GROUP
    dmixed = column(turned(col_inv), arrived, "column_in_t")
    all_dmixed = lax.all_gather(dmixed, "dp")
    sent = call(
        turn_kernel, shaped((height, wide)), "turn", 60,
        in_specs=[WHOLE] * 5 + [HBM], out_specs=WHOLE,
        scratch_shapes=[
            pltpu.VMEM((modes, spectral_weight.shape[2]), BF16),
            pltpu.VMEM((modes, LANES), F32),
            pltpu.VMEM((modes, LANES), F32),
            pltpu.VMEM((modes, LANES), F32),
            pltpu.VMEM((modes_x, wide), BF16),
            sems(modes // (2 * LANES)),
        ],
    )(
        dmixed, order_in, order_out, turned(col_fwd), jnp.asarray(summed),
        gathered.reshape(modes, spectral_weight.shape[2]),
    )
    back = across(sent, "pencil").reshape(sent_shape)
    own = spectral_weight.shape[0]
    own_dmixed = lax.dynamic_slice_in_dim(all_dmixed, own * lax.axis_index("dp"), own, axis=1)
    grad_weight = call(
        grad_kernel, shaped((GROUP, GROUP, channels, 2 * channels), F32), "weight_grad",
        in_specs=[WHOLE] * 3 + [HBM], out_specs=WHOLE,
    )(spectrum, own_dmixed.reshape(modes_x, wide), order_in, sent)
    grad_input = call(
        row_out_kernel, shaped(field_shape), "row_out", 60,
        in_specs=[HBM, WHOLE, HBM], out_specs=HBM,
        scratch_shapes=buffers(field_shape, narrow, field_shape)
        + [sems(chunks + 1), sems(chunks)],
    )(dpre, back, jnp.asarray(row_fwd_t))
    return (grad_input[None], grad_weight.reshape(spectral_weight.shape))


def solution(mesh):
    return jax.shard_map(
        local,
        mesh=mesh,
        in_specs=(
            P("dp", None, "pencil", None),
            P("dp", None, "pencil", None),
            P("dp", "pencil", None),
        ),
        out_specs=(P("dp", None, "pencil", None), P("dp", "pencil", None)),
        check_vma=False,
    )
```

```python
import functools
import math

import jax
import jax.numpy as jnp
import ml_dtypes
import numpy as np
from jax import lax
from jax.experimental import pallas as pl
from jax.experimental.pallas import tpu as pltpu
from jax.sharding import PartitionSpec as P

BF16 = jnp.bfloat16
F32 = jnp.float32
LANES = 128
GROUP = 8
SLABS = 16
CHUNK = 8
TILE = 256
MIB = 1024 * 1024


def row_tables(columns, modes):
    k = np.arange(modes, dtype=np.int64)
    y = np.arange(columns, dtype=np.int64)
    phases = (k[:, None] * y[None, :] % columns).astype(np.float32) * np.float32(
        2.0 * math.pi / columns
    )
    paired = np.stack([np.cos(phases), -np.sin(phases)], axis=0)
    forward = (paired / np.float32(math.sqrt(columns))).reshape(2 * modes, columns)
    factor = np.where(k == 0, 1.0, 2.0).astype(np.float32) / np.float32(math.sqrt(2 * modes))
    inverse = (paired * factor[None, :, None]).reshape(2 * modes, columns)
    return forward.astype(ml_dtypes.bfloat16), inverse.astype(ml_dtypes.bfloat16)


def column_tables(rows, modes):
    j = np.arange(modes, dtype=np.int64)
    f = np.where(j < modes // 2, j, rows - modes + j)
    x = np.arange(rows, dtype=np.int64)
    phases = (f[:, None] * x[None, :] % rows).astype(np.float32) * np.float32(2.0 * math.pi / rows)
    c, s = np.cos(phases), np.sin(phases)
    forward = np.block([[c, s], [-s, c]]) / np.float32(math.sqrt(rows))
    inverse = np.block([[c.T, -s.T], [s.T, c.T]]) / np.float32(math.sqrt(modes))
    return forward.astype(ml_dtypes.bfloat16), inverse.astype(ml_dtypes.bfloat16)


def mode_order(channels, parts=2):
    half = channels // 2
    table = np.zeros((parts * channels * GROUP, parts * channels * GROUP), np.float32)
    for c in range(channels):
        for p in range(parts):
            for k in range(GROUP):
                source = ((c // half * parts + p) * half + c % half) * GROUP + k
                table[source, (k * parts + p) * channels + c] = 1.0
    return table.astype(ml_dtypes.bfloat16)


def dot(a, b):
    return jnp.dot(a, b, preferred_element_type=F32)


def dot_t(a, b):
    return lax.dot_general(a, b, (((1,), (1,)), ((), ())), preferred_element_type=F32)


def swap_groups(slabs):
    group = lax.broadcasted_iota(jnp.int32, slabs[0].shape, 1) // GROUP
    bit = 1
    while bit < SLABS:
        low = (group & bit) == 0
        out = list(slabs)
        for i in range(SLABS):
            if i & bit:
                continue
            a, b = slabs[i], slabs[i | bit]
            out[i] = jnp.where(low, a, pltpu.roll(b, bit * GROUP, 1))
            out[i | bit] = jnp.where(low, pltpu.roll(a, LANES - bit * GROUP, 1), b)
        slabs = out
        bit *= 2
    return slabs


def pack(spec, out_ref, half):
    rows = out_ref.shape[1]
    for p in range(2):
        slabs = [
            spec[c * rows : (c + 1) * rows, p * LANES : (p + 1) * LANES] for c in range(SLABS)
        ]
        at = (2 * half + p) * LANES
        for d, slab in enumerate(swap_groups(slabs)):
            out_ref[d, :, at : at + LANES] = slab.astype(BF16)


def unpack(in_ref, half):
    parts = []
    for p in range(2):
        at = (2 * half + p) * LANES
        slabs = [in_ref[d, :, at : at + LANES].astype(F32) for d in range(SLABS)]
        parts.append(jnp.concatenate(swap_groups(slabs), axis=0).astype(BF16))
    return jnp.concatenate(parts, axis=1)


def slope(v):
    e = jnp.exp2((-0.5 / math.log(2.0)) * (v * v)).astype(BF16)
    v = v.astype(BF16)

    def c(value):
        return jnp.asarray(value, BF16)

    a = jnp.abs(v)
    t = c(1.0) / (c(1.0) + c(0.3275911 / math.sqrt(2.0)) * a)
    q = c(0.5 * 1.061405429) * t - c(0.5 * 1.453152027)
    q = q * t + c(0.5 * 1.421413741)
    q = q * t - c(0.5 * 0.284496736)
    q = q * t + c(0.5 * 0.254829592)
    g = e * (a * c(1.0 / math.sqrt(2.0 * math.pi)) - q * t)
    return jnp.where(v < c(0.0), -g, c(1.0) + g)


def flat(block):
    return block.reshape(block.shape[0] * block.shape[1], block.shape[-1])


def load(source, target, sem):
    copy = pltpu.make_async_copy(source, target, sem)
    copy.start()
    return copy


def chunk(i):
    return pl.ds(i * CHUNK, CHUNK)


def row_in_kernel(field_hbm, table_hbm, out_ref, field_ref, table_ref, sems):
    chunks = field_ref.shape[0] // CHUNK
    first = load(table_hbm, table_ref, sems.at[chunks])
    copies = [
        load(field_hbm.at[chunk(i)], field_ref.at[chunk(i)], sems.at[i]) for i in range(chunks)
    ]
    first.wait()
    parts = []
    for i in range(chunks):
        copies[i].wait()
        parts.append(dot(flat(field_ref[i * CHUNK : (i + 1) * CHUNK]), table_ref[...]))
    per_half = SLABS // CHUNK
    for h in range(2):
        pack(jnp.concatenate(parts[h * per_half : (h + 1) * per_half], axis=0), out_ref, h)


def middle_kernel(field_ref, cot_ref, back_ref, inv_ref, dpre_ref, out_ref):
    rows, columns = field_ref.shape[1:]
    tall = SLABS * rows
    cuts = [slice(y, y + TILE) for y in range(0, columns, TILE)]
    for h in range(2):
        at = slice(h * SLABS, (h + 1) * SLABS)
        back = unpack(back_ref, h)
        total = jnp.zeros((tall, out_ref.shape[2] // 2), F32)
        branch = dot(back, inv_ref[:, cuts[0]])
        held = None
        for m, cut in enumerate(cuts):
            following = dot(back, inv_ref[:, cuts[m + 1]]) if m + 1 < len(cuts) else None
            pre = flat(field_ref[at, :, cut]).astype(F32) + branch
            dpre = (flat(cot_ref[at, :, cut]) * slope(pre)).astype(BF16)
            if held is not None:
                total = total + dot_t(held, inv_ref[:, cuts[m - 1]])
            dpre_ref[at, :, cut] = dpre.reshape(SLABS, rows, TILE)
            held, branch = dpre, following
        total = total + dot_t(held, inv_ref[:, cuts[-1]])
        pack(total, out_ref, h)


def row_out_kernel(
    dpre_hbm, back_ref, table_ref, out_hbm, dpre_ref, out_ref, sems, sent_sems
):
    chunks = dpre_ref.shape[0] // CHUNK
    rows, columns = dpre_ref.shape[1:]
    per_half = SLABS // CHUNK
    loads = [
        load(dpre_hbm.at[chunk(i)], dpre_ref.at[chunk(i)], sems.at[i]) for i in range(chunks)
    ]
    stores = []
    for h in range(2):
        back = unpack(back_ref, h)
        for n in range(per_half):
            i = h * per_half + n
            loads[i].wait()
            left = back[n * CHUNK * rows : (n + 1) * CHUNK * rows]
            at = slice(i * CHUNK, (i + 1) * CHUNK)
            for start in range(0, columns, TILE):
                cut = slice(start, start + TILE)
                value = flat(dpre_ref[at, :, cut]).astype(F32) + dot(left, table_ref[:, cut])
                out_ref[at, :, cut] = value.astype(BF16).reshape(CHUNK, rows, TILE)
            stores.append(load(out_ref.at[chunk(i)], out_hbm.at[chunk(i)], sent_sems.at[i]))
    for copy in stores:
        copy.wait()


def stack_parts(values):
    return jnp.concatenate(
        [
            jnp.concatenate(
                [values[:, (2 * h + p) * LANES : (2 * h + p + 1) * LANES] for h in range(2)], axis=1
            )
            for p in range(2)
        ],
        axis=0,
    )


def lay_parts(result, out_ref):
    rows = out_ref.shape[0]
    for h in range(2):
        for p in range(2):
            at = (2 * h + p) * LANES
            out_ref[:, at : at + LANES] = result[
                p * rows : (p + 1) * rows, h * LANES : (h + 1) * LANES
            ]


def column_kernel(table_ref, in_ref, *early_and_out):
    out_ref = early_and_out[-1]
    lay_parts(dot(table_ref[...], stack_parts(in_ref[...])).astype(BF16), out_ref)


def weight_kernel(in_ref, out_ref):
    modes, channels = in_ref.shape[0], in_ref.shape[2]
    zero = jnp.zeros((2 * channels, 2 * channels), F32)
    for j in range(modes):
        for pair in range(GROUP // 2):
            blocks = []
            for i in range(2):
                w = in_ref[j, 2 * pair + i].astype(F32)
                turned = jnp.concatenate([-w[:, channels:], w[:, :channels]], axis=1)
                block = jnp.concatenate([w, turned], axis=0)
                blocks.append(
                    jnp.concatenate([block, zero] if i == 0 else [zero, block], axis=1)
                )
            out_ref[pair, :, j * LANES : (j + 1) * LANES] = jnp.concatenate(blocks, axis=0).astype(
                BF16
            )


def own_row(shape, axis):
    return lax.broadcasted_iota(jnp.int32, shape, axis) % GROUP


def mix_kernel(transposed, in_ref, weight_ref, order_ref, order_t_ref, out_ref):
    values = dot(in_ref[...], order_ref[...]).astype(BF16)
    rows = values.shape[0]
    own = own_row((rows, LANES), 0)
    pieces = []
    for pair in range(GROUP // 2):
        left = values[:, pair * LANES : (pair + 1) * LANES]
        total = jnp.zeros((rows, LANES), F32)
        for j in range(GROUP):
            weight = weight_ref[pair, :, j * LANES : (j + 1) * LANES]
            term = dot_t(left, weight) if transposed else dot(left, weight)
            total = jnp.where(own == j, term, total)
        pieces.append(total.astype(BF16))
    mixed = jnp.concatenate(pieces, axis=1)
    out_ref[...] = dot(mixed, order_t_ref[...]).astype(BF16)


def grad_kernel(spec_ref, dmixed_ref, order_ref, after_hbm, early_ref, out_ref):
    spec = dot(spec_ref[...], order_ref[...])
    dmixed = dot(dmixed_ref[...], order_ref[...]).astype(BF16)
    rows = spec.shape[0]
    channels = out_ref.shape[2]
    own = own_row((LANES, rows), 1)
    for pair in range(GROUP // 2):
        left = spec[:, pair * LANES : (pair + 1) * LANES].T
        right = dmixed[:, pair * LANES : (pair + 1) * LANES]
        for j in range(GROUP):
            outer = dot(jnp.where(own == j, left, 0.0).astype(BF16), right)
            for i in range(2):
                at = 2 * channels * i
                re = outer[at : at + channels, at : at + 2 * channels]
                im = outer[at + channels : at + 2 * channels, at : at + 2 * channels]
                turned = jnp.concatenate([im[:, channels:], -im[:, :channels]], axis=1)
                out_ref[j, 2 * pair + i] = re + turned


def shaped(shape, dtype=BF16):
    return jax.ShapeDtypeStruct(shape, dtype)


def call(kernel, out, name, vmem=16, **kw):
    return pl.pallas_call(
        kernel,
        out_shape=out,
        name=name,
        compiler_params=pltpu.CompilerParams(vmem_limit_bytes=vmem * MIB),
        **kw,
    )


HBM = pl.BlockSpec(memory_space=pltpu.HBM)
WHOLE = pl.BlockSpec(memory_space=pltpu.VMEM)


def buffers(*shapes):
    return [pltpu.VMEM(shape, BF16) for shape in shapes]


def sems(count):
    return pltpu.SemaphoreType.DMA((count,))


def across(values, axis):
    return lax.all_to_all(values, axis, split_axis=0, concat_axis=0, tiled=True)


def local(field_in, cotangent, spectral_weight):
    channels, rows_here, columns = field_in.shape[1:]
    pencils = lax.axis_size("pencil")
    modes_y = spectral_weight.shape[1] * pencils
    modes_x = spectral_weight.shape[0] * lax.axis_size("dp")
    height = rows_here * pencils
    wide = 4 * LANES
    chunks = channels // CHUNK
    row_fwd_t, row_inv = row_tables(columns, modes_y)
    col_fwd, col_inv = column_tables(height, modes_x)
    order = mode_order(channels)
    field = field_in[0]
    cot = cotangent[0]
    field_shape = field.shape
    sent_shape = (SLABS, rows_here, wide)
    tall = (columns, 2 * modes_y)
    inv_table, row_table = jnp.asarray(row_inv), jnp.asarray(row_fwd_t)

    def turned(table):
        return jnp.asarray(np.ascontiguousarray(table.T))

    def column(table, values, name, *early):
        return call(column_kernel, shaped((table.shape[0] // 2, wide)), name)(
            table, values, *early
        )

    weights = call(
        weight_kernel, shaped((GROUP // 2, LANES, GROUP * LANES)), "weight_blocks"
    )(spectral_weight.reshape(GROUP, GROUP, channels, 2 * channels))
    order_in, order_out = jnp.asarray(order), turned(order)

    def mix(values, transposed, name):
        kernel = functools.partial(mix_kernel, transposed)
        mixed = call(kernel, shaped((modes_x, wide)), name)(values, weights, order_in, order_out)
        return across(mixed, "dp")

    sent = call(
        row_in_kernel, shaped(sent_shape), "row_in", 60,
        in_specs=[HBM] * 2, out_specs=WHOLE,
        scratch_shapes=buffers(field_shape, tall) + [sems(chunks + 1)],
    )(field, turned(row_fwd_t))
    arrived = across(sent, "pencil").reshape(height, wide)
    spectrum = across(column(jnp.asarray(col_fwd), arrived, "column_in"), "dp")
    mixed = mix(spectrum, False, "mix")
    back = across(column(jnp.asarray(col_inv), mixed, "column_out", inv_table), "pencil")
    dpre, sent = call(
        middle_kernel, [shaped(field_shape), shaped(sent_shape)], "middle", 24,
        in_specs=[WHOLE] * 4, out_specs=[WHOLE] * 2,
    )(field, cot, back.reshape(sent_shape), inv_table)
    arrived = across(sent, "pencil").reshape(height, wide)
    dmixed = across(column(turned(col_inv), arrived, "column_in_t"), "dp")
    sent = column(turned(col_fwd), mix(dmixed, True, "mix_t"), "column_out_t")
    back = across(sent, "pencil").reshape(sent_shape)
    grad_weight = call(
        grad_kernel, shaped((GROUP, GROUP, channels, 2 * channels), F32), "weight_grad",
        in_specs=[WHOLE] * 3 + [HBM, WHOLE], out_specs=WHOLE,
    )(spectrum, dmixed, order_in, sent, row_table)
    grad_input = call(
        row_out_kernel, shaped(field_shape), "row_out", 52,
        in_specs=[HBM, WHOLE, WHOLE], out_specs=HBM,
        scratch_shapes=buffers(field_shape, field_shape) + [sems(chunks)] * 2,
    )(dpre, back, row_table)
    return (grad_input[None], grad_weight.reshape(spectral_weight.shape))


def solution(mesh):
    return jax.shard_map(
        local,
        mesh=mesh,
        in_specs=(
            P("dp", None, "pencil", None),
            P("dp", None, "pencil", None),
            P("dp", "pencil", None),
        ),
        out_specs=(P("dp", None, "pencil", None), P("dp", "pencil", None)),
        check_vma=False,
    )
```

```python
import functools
import math

import jax
import jax.numpy as jnp
import ml_dtypes
import numpy as np
from jax import lax
from jax.experimental import pallas as pl
from jax.experimental.pallas import tpu as pltpu
from jax.sharding import PartitionSpec as P

BF16 = jnp.bfloat16
F32 = jnp.float32
LANES = 128
GROUP = 8
SLABS = 16
CHUNK = 8
TILE = 256
MIB = 1024 * 1024


def row_tables(columns, modes):
    k = np.arange(modes, dtype=np.int64)
    y = np.arange(columns, dtype=np.int64)
    phases = (k[:, None] * y[None, :] % columns).astype(np.float32) * np.float32(
        2.0 * math.pi / columns
    )
    paired = np.stack([np.cos(phases), -np.sin(phases)], axis=0)
    forward = (paired / np.float32(math.sqrt(columns))).reshape(2 * modes, columns)
    factor = np.where(k == 0, 1.0, 2.0).astype(np.float32) / np.float32(math.sqrt(2 * modes))
    inverse = (paired * factor[None, :, None]).reshape(2 * modes, columns)
    return forward.astype(ml_dtypes.bfloat16), inverse.astype(ml_dtypes.bfloat16)


def column_tables(rows, modes):
    j = np.arange(modes, dtype=np.int64)
    f = np.where(j < modes // 2, j, rows - modes + j)
    x = np.arange(rows, dtype=np.int64)
    phases = (f[:, None] * x[None, :] % rows).astype(np.float32) * np.float32(2.0 * math.pi / rows)
    c, s = np.cos(phases), np.sin(phases)
    forward = np.block([[c, s], [-s, c]]) / np.float32(math.sqrt(rows))
    inverse = np.block([[c.T, -s.T], [s.T, c.T]]) / np.float32(math.sqrt(modes))
    return forward.astype(ml_dtypes.bfloat16), inverse.astype(ml_dtypes.bfloat16)


def mode_order(channels, parts=2):
    half = channels // 2
    table = np.zeros((parts * channels * GROUP, parts * channels * GROUP), np.float32)
    for c in range(channels):
        for p in range(parts):
            for k in range(GROUP):
                source = ((c // half * parts + p) * half + c % half) * GROUP + k
                table[source, (k * parts + p) * channels + c] = 1.0
    return table.astype(ml_dtypes.bfloat16)


def dot(a, b):
    return jnp.dot(a, b, preferred_element_type=F32)


def dot_t(a, b):
    return lax.dot_general(a, b, (((1,), (1,)), ((), ())), preferred_element_type=F32)


def swap_groups(slabs):
    group = lax.broadcasted_iota(jnp.int32, slabs[0].shape, 1) // GROUP
    bit = 1
    while bit < SLABS:
        low = (group & bit) == 0
        out = list(slabs)
        for i in range(SLABS):
            if i & bit:
                continue
            a, b = slabs[i], slabs[i | bit]
            out[i] = jnp.where(low, a, pltpu.roll(b, bit * GROUP, 1))
            out[i | bit] = jnp.where(low, pltpu.roll(a, LANES - bit * GROUP, 1), b)
        slabs = out
        bit *= 2
    return slabs


def pack(spec, out_ref, half):
    rows = out_ref.shape[1]
    for p in range(2):
        slabs = [
            spec[c * rows : (c + 1) * rows, p * LANES : (p + 1) * LANES] for c in range(SLABS)
        ]
        at = (2 * half + p) * LANES
        for d, slab in enumerate(swap_groups(slabs)):
            out_ref[d, :, at : at + LANES] = slab.astype(BF16)


def unpack(in_ref, half):
    parts = []
    for p in range(2):
        at = (2 * half + p) * LANES
        slabs = [in_ref[d, :, at : at + LANES].astype(F32) for d in range(SLABS)]
        parts.append(jnp.concatenate(swap_groups(slabs), axis=0).astype(BF16))
    return jnp.concatenate(parts, axis=1)


def slope(v):
    e = jnp.exp2((-0.5 / math.log(2.0)) * (v * v)).astype(BF16)
    v = v.astype(BF16)

    def c(value):
        return jnp.asarray(value, BF16)

    a = jnp.abs(v)
    t = c(1.0) / (c(1.0) + c(0.3275911 / math.sqrt(2.0)) * a)
    q = c(0.5 * 1.061405429) * t - c(0.5 * 1.453152027)
    q = q * t + c(0.5 * 1.421413741)
    q = q * t - c(0.5 * 0.284496736)
    q = q * t + c(0.5 * 0.254829592)
    g = e * (a * c(1.0 / math.sqrt(2.0 * math.pi)) - q * t)
    return jnp.where(v < c(0.0), -g, c(1.0) + g)


def flat(block):
    return block.reshape(block.shape[0] * block.shape[1], block.shape[-1])


def load(source, target, sem):
    copy = pltpu.make_async_copy(source, target, sem)
    copy.start()
    return copy


def chunk(i):
    return pl.ds(i * CHUNK, CHUNK)


def row_in_kernel(field_hbm, table_hbm, out_ref, field_ref, table_ref, sems):
    chunks = field_ref.shape[0] // CHUNK
    first = load(table_hbm, table_ref, sems.at[chunks])
    copies = [
        load(field_hbm.at[chunk(i)], field_ref.at[chunk(i)], sems.at[i]) for i in range(chunks)
    ]
    first.wait()
    parts = []
    for i in range(chunks):
        copies[i].wait()
        parts.append(dot(flat(field_ref[i * CHUNK : (i + 1) * CHUNK]), table_ref[...]))
    per_half = SLABS // CHUNK
    for h in range(2):
        pack(jnp.concatenate(parts[h * per_half : (h + 1) * per_half], axis=0), out_ref, h)


def middle_kernel(
    field_ref, cot_hbm, back_ref, inv_ref, dpre_ref, out_ref, cot_ref, sems
):
    rows, columns = field_ref.shape[1:]
    tall = SLABS * rows
    halves = [pl.ds(h * SLABS, SLABS) for h in range(2)]
    loads = [load(cot_hbm.at[at], cot_ref.at[at], sems.at[h]) for h, at in enumerate(halves)]
    cuts = [slice(y, y + TILE) for y in range(0, columns, TILE)]
    for h in range(2):
        at = slice(h * SLABS, (h + 1) * SLABS)
        back = unpack(back_ref, h)
        total = jnp.zeros((tall, out_ref.shape[2] // 2), F32)
        branch = dot(back, inv_ref[:, cuts[0]])
        loads[h].wait()
        held = None
        for m, cut in enumerate(cuts):
            following = dot(back, inv_ref[:, cuts[m + 1]]) if m + 1 < len(cuts) else None
            pre = flat(field_ref[at, :, cut]).astype(F32) + branch
            dpre = (flat(cot_ref[at, :, cut]) * slope(pre)).astype(BF16)
            if held is not None:
                total = total + dot_t(held, inv_ref[:, cuts[m - 1]])
            dpre_ref[at, :, cut] = dpre.reshape(SLABS, rows, TILE)
            held, branch = dpre, following
        total = total + dot_t(held, inv_ref[:, cuts[-1]])
        pack(total, out_ref, h)


def row_out_kernel(
    dpre_hbm, back_ref, table_ref, out_hbm, dpre_ref, out_ref, sems, sent_sems
):
    chunks = dpre_ref.shape[0] // CHUNK
    rows, columns = dpre_ref.shape[1:]
    per_half = SLABS // CHUNK
    loads = [
        load(dpre_hbm.at[chunk(i)], dpre_ref.at[chunk(i)], sems.at[i]) for i in range(chunks)
    ]
    stores = []
    for h in range(2):
        back = unpack(back_ref, h)
        for n in range(per_half):
            i = h * per_half + n
            loads[i].wait()
            left = back[n * CHUNK * rows : (n + 1) * CHUNK * rows]
            at = slice(i * CHUNK, (i + 1) * CHUNK)
            for start in range(0, columns, TILE):
                cut = slice(start, start + TILE)
                value = flat(dpre_ref[at, :, cut]).astype(F32) + dot(left, table_ref[:, cut])
                out_ref[at, :, cut] = value.astype(BF16).reshape(CHUNK, rows, TILE)
            stores.append(load(out_ref.at[chunk(i)], out_hbm.at[chunk(i)], sent_sems.at[i]))
    for copy in stores:
        copy.wait()


def stack_parts(values):
    return jnp.concatenate(
        [
            jnp.concatenate(
                [values[:, (2 * h + p) * LANES : (2 * h + p + 1) * LANES] for h in range(2)], axis=1
            )
            for p in range(2)
        ],
        axis=0,
    )


def lay_parts(result, out_ref):
    rows = out_ref.shape[0]
    for h in range(2):
        for p in range(2):
            at = (2 * h + p) * LANES
            out_ref[:, at : at + LANES] = result[
                p * rows : (p + 1) * rows, h * LANES : (h + 1) * LANES
            ]


def column_kernel(table_ref, in_ref, *early_and_out):
    out_ref = early_and_out[-1]
    lay_parts(dot(table_ref[...], stack_parts(in_ref[...])).astype(BF16), out_ref)


def weight_kernel(in_ref, *early_and_out):
    out_ref = early_and_out[-1]
    modes, channels = in_ref.shape[0], in_ref.shape[2]
    zero = jnp.zeros((2 * channels, 2 * channels), F32)
    for j in range(modes):
        for pair in range(GROUP // 2):
            blocks = []
            for i in range(2):
                w = in_ref[j, 2 * pair + i].astype(F32)
                turned = jnp.concatenate([-w[:, channels:], w[:, :channels]], axis=1)
                block = jnp.concatenate([w, turned], axis=0)
                blocks.append(
                    jnp.concatenate([block, zero] if i == 0 else [zero, block], axis=1)
                )
            out_ref[pair, :, j * LANES : (j + 1) * LANES] = jnp.concatenate(blocks, axis=0).astype(
                BF16
            )


def own_row(shape, axis):
    return lax.broadcasted_iota(jnp.int32, shape, axis) % GROUP


def mix_kernel(transposed, in_ref, weight_ref, order_ref, order_t_ref, out_ref):
    values = dot(in_ref[...], order_ref[...]).astype(BF16)
    rows = values.shape[0]
    own = own_row((rows, LANES), 0)
    pieces = []
    for pair in range(GROUP // 2):
        left = values[:, pair * LANES : (pair + 1) * LANES]
        total = jnp.zeros((rows, LANES), F32)
        for j in range(GROUP):
            weight = weight_ref[pair, :, j * LANES : (j + 1) * LANES]
            term = dot_t(left, weight) if transposed else dot(left, weight)
            total = jnp.where(own == j, term, total)
        pieces.append(total.astype(BF16))
    mixed = jnp.concatenate(pieces, axis=1)
    out_ref[...] = dot(mixed, order_t_ref[...]).astype(BF16)


def grad_kernel(spec_ref, dmixed_ref, order_ref, after_hbm, early_ref, out_ref):
    spec = dot(spec_ref[...], order_ref[...])
    dmixed = dot(dmixed_ref[...], order_ref[...]).astype(BF16)
    rows = spec.shape[0]
    channels = out_ref.shape[2]
    own = own_row((LANES, rows), 1)
    for pair in range(GROUP // 2):
        left = spec[:, pair * LANES : (pair + 1) * LANES].T
        right = dmixed[:, pair * LANES : (pair + 1) * LANES]
        for j in range(GROUP):
            outer = dot(jnp.where(own == j, left, 0.0).astype(BF16), right)
            for i in range(2):
                at = 2 * channels * i
                re = outer[at : at + channels, at : at + 2 * channels]
                im = outer[at + channels : at + 2 * channels, at : at + 2 * channels]
                turned = jnp.concatenate([im[:, channels:], -im[:, :channels]], axis=1)
                out_ref[j, 2 * pair + i] = re + turned


def shaped(shape, dtype=BF16):
    return jax.ShapeDtypeStruct(shape, dtype)


def call(kernel, out, name, vmem=16, **kw):
    return pl.pallas_call(
        kernel,
        out_shape=out,
        name=name,
        compiler_params=pltpu.CompilerParams(vmem_limit_bytes=vmem * MIB),
        **kw,
    )


HBM = pl.BlockSpec(memory_space=pltpu.HBM)
WHOLE = pl.BlockSpec(memory_space=pltpu.VMEM)


def buffers(*shapes):
    return [pltpu.VMEM(shape, BF16) for shape in shapes]


def sems(count):
    return pltpu.SemaphoreType.DMA((count,))


def across(values, axis):
    return lax.all_to_all(values, axis, split_axis=0, concat_axis=0, tiled=True)


def local(field_in, cotangent, spectral_weight):
    channels, rows_here, columns = field_in.shape[1:]
    pencils = lax.axis_size("pencil")
    modes_y = spectral_weight.shape[1] * pencils
    modes_x = spectral_weight.shape[0] * lax.axis_size("dp")
    height = rows_here * pencils
    wide = 4 * LANES
    chunks = channels // CHUNK
    row_fwd_t, row_inv = row_tables(columns, modes_y)
    col_fwd, col_inv = column_tables(height, modes_x)
    order = mode_order(channels)
    field = field_in[0]
    cot = cotangent[0]
    field_shape = field.shape
    sent_shape = (SLABS, rows_here, wide)
    tall = (columns, 2 * modes_y)
    inv_table, row_table = jnp.asarray(row_inv), jnp.asarray(row_fwd_t)

    def turned(table):
        return jnp.asarray(np.ascontiguousarray(table.T))

    def column(table, values, name, *early):
        return call(column_kernel, shaped((table.shape[0] // 2, wide)), name)(
            table, values, *early
        )

    order_in, order_out = jnp.asarray(order), turned(order)
    fwd_table, col_table = jnp.asarray(col_fwd), jnp.asarray(col_inv)
    weights = call(
        weight_kernel, shaped((GROUP // 2, LANES, GROUP * LANES)), "weight_blocks"
    )(
        spectral_weight.reshape(GROUP, GROUP, channels, 2 * channels),
        order_in, order_out, col_table,
    )

    def mix(values, transposed, name):
        kernel = functools.partial(mix_kernel, transposed)
        mixed = call(kernel, shaped((modes_x, wide)), name)(values, weights, order_in, order_out)
        return across(mixed, "dp")

    sent = call(
        row_in_kernel, shaped(sent_shape), "row_in", 60,
        in_specs=[HBM] * 2, out_specs=WHOLE,
        scratch_shapes=buffers(field_shape, tall) + [sems(chunks + 1)],
    )(field, turned(row_fwd_t))
    arrived = across(sent, "pencil").reshape(height, wide)
    modes = column(fwd_table, arrived, "column_in", weights)
    spectrum = across(modes, "dp")
    mixed = mix(spectrum, False, "mix")
    back = across(column(col_table, mixed, "column_out", inv_table), "pencil")
    dpre, sent = call(
        middle_kernel, [shaped(field_shape), shaped(sent_shape)], "middle", 40,
        in_specs=[WHOLE, HBM, WHOLE, WHOLE], out_specs=[WHOLE] * 2,
        scratch_shapes=buffers(field_shape) + [sems(2)],
    )(field, cot, back.reshape(sent_shape), inv_table)
    arrived = across(sent, "pencil").reshape(height, wide)
    dmixed = across(column(turned(col_inv), arrived, "column_in_t"), "dp")
    sent = column(turned(col_fwd), mix(dmixed, True, "mix_t"), "column_out_t")
    back = across(sent, "pencil").reshape(sent_shape)
    grad_weight = call(
        grad_kernel, shaped((GROUP, GROUP, channels, 2 * channels), F32), "weight_grad",
        in_specs=[WHOLE] * 3 + [HBM, WHOLE], out_specs=WHOLE,
    )(spectrum, dmixed, order_in, sent, row_table)
    grad_input = call(
        row_out_kernel, shaped(field_shape), "row_out", 52,
        in_specs=[HBM, WHOLE, WHOLE], out_specs=HBM,
        scratch_shapes=buffers(field_shape, field_shape) + [sems(chunks)] * 2,
    )(dpre, back, row_table)
    return (grad_input[None], grad_weight.reshape(spectral_weight.shape))


def solution(mesh):
    return jax.shard_map(
        local,
        mesh=mesh,
        in_specs=(
            P("dp", None, "pencil", None),
            P("dp", None, "pencil", None),
            P("dp", "pencil", None),
        ),
        out_specs=(P("dp", None, "pencil", None), P("dp", "pencil", None)),
        check_vma=False,
    )
```

```python
import functools
import math

import jax
import jax.numpy as jnp
import ml_dtypes
import numpy as np
from jax import lax
from jax.experimental import pallas as pl
from jax.experimental.pallas import tpu as pltpu
from jax.sharding import PartitionSpec as P

BF16 = jnp.bfloat16
F32 = jnp.float32
LANES = 128
GROUP = 8
SLABS = 16
CHUNK = 8
TILE = 256
MIB = 1024 * 1024


def row_tables(columns, modes):
    k = np.arange(modes, dtype=np.int64)
    y = np.arange(columns, dtype=np.int64)
    phases = (k[:, None] * y[None, :] % columns).astype(np.float32) * np.float32(
        2.0 * math.pi / columns
    )
    paired = np.stack([np.cos(phases), -np.sin(phases)], axis=0)
    forward = (paired / np.float32(math.sqrt(columns))).reshape(2 * modes, columns)
    factor = np.where(k == 0, 1.0, 2.0).astype(np.float32) / np.float32(math.sqrt(2 * modes))
    inverse = (paired * factor[None, :, None]).reshape(2 * modes, columns)
    return forward.astype(ml_dtypes.bfloat16), inverse.astype(ml_dtypes.bfloat16)


def column_tables(rows, modes):
    j = np.arange(modes, dtype=np.int64)
    f = np.where(j < modes // 2, j, rows - modes + j)
    x = np.arange(rows, dtype=np.int64)
    phases = (f[:, None] * x[None, :] % rows).astype(np.float32) * np.float32(2.0 * math.pi / rows)
    c, s = np.cos(phases), np.sin(phases)
    forward = np.block([[c, s], [-s, c]]) / np.float32(math.sqrt(rows))
    inverse = np.block([[c.T, -s.T], [s.T, c.T]]) / np.float32(math.sqrt(modes))
    return forward.astype(ml_dtypes.bfloat16), inverse.astype(ml_dtypes.bfloat16)


def mode_order(channels, parts=2):
    half = channels // 2
    table = np.zeros((parts * channels * GROUP, parts * channels * GROUP), np.float32)
    for c in range(channels):
        for p in range(parts):
            for k in range(GROUP):
                source = ((c // half * parts + p) * half + c % half) * GROUP + k
                table[source, (k * parts + p) * channels + c] = 1.0
    return table.astype(ml_dtypes.bfloat16)


def dot(a, b):
    return jnp.dot(a, b, preferred_element_type=F32)


def dot_t(a, b):
    return lax.dot_general(a, b, (((1,), (1,)), ((), ())), preferred_element_type=F32)


def swap_groups(slabs):
    group = lax.broadcasted_iota(jnp.int32, slabs[0].shape, 1) // GROUP
    bit = 1
    while bit < SLABS:
        low = (group & bit) == 0
        out = list(slabs)
        for i in range(SLABS):
            if i & bit:
                continue
            a, b = slabs[i], slabs[i | bit]
            out[i] = jnp.where(low, a, pltpu.roll(b, bit * GROUP, 1))
            out[i | bit] = jnp.where(low, pltpu.roll(a, LANES - bit * GROUP, 1), b)
        slabs = out
        bit *= 2
    return slabs


def pack(spec, out_ref, half):
    rows = out_ref.shape[1]
    for p in range(2):
        slabs = [
            spec[c * rows : (c + 1) * rows, p * LANES : (p + 1) * LANES] for c in range(SLABS)
        ]
        at = (2 * half + p) * LANES
        for d, slab in enumerate(swap_groups(slabs)):
            out_ref[d, :, at : at + LANES] = slab.astype(BF16)


def unpack(in_ref, half):
    parts = []
    for p in range(2):
        at = (2 * half + p) * LANES
        slabs = [in_ref[d, :, at : at + LANES].astype(F32) for d in range(SLABS)]
        parts.append(jnp.concatenate(swap_groups(slabs), axis=0).astype(BF16))
    return jnp.concatenate(parts, axis=1)


def slope(v):
    e = jnp.exp2((-0.5 / math.log(2.0)) * (v * v)).astype(BF16)
    v = v.astype(BF16)

    def c(value):
        return jnp.asarray(value, BF16)

    a = jnp.abs(v)
    t = c(1.0) / (c(1.0) + c(0.3275911 / math.sqrt(2.0)) * a)
    q = c(0.5 * 1.061405429) * t - c(0.5 * 1.453152027)
    q = q * t + c(0.5 * 1.421413741)
    q = q * t - c(0.5 * 0.284496736)
    q = q * t + c(0.5 * 0.254829592)
    g = e * (a * c(1.0 / math.sqrt(2.0 * math.pi)) - q * t)
    return jnp.where(v < c(0.0), -g, c(1.0) + g)


def flat(block):
    return block.reshape(block.shape[0] * block.shape[1], block.shape[-1])


def load(source, target, sem):
    copy = pltpu.make_async_copy(source, target, sem)
    copy.start()
    return copy


def chunk(i):
    return pl.ds(i * CHUNK, CHUNK)


def row_in_kernel(field_hbm, table_hbm, out_ref, field_ref, table_ref, sems):
    first = load(table_hbm, table_ref, sems.at[2])
    halves = [pl.ds(h * SLABS, SLABS) for h in range(2)]
    copies = [
        load(field_hbm.at[at], field_ref.at[at], sems.at[h]) for h, at in enumerate(halves)
    ]
    first.wait()
    parts = []
    for h, at in enumerate(halves):
        copies[h].wait()
        parts.append(dot(flat(field_ref[at]), table_ref[...]))
    for h in range(2):
        pack(parts[h], out_ref, h)


def middle_kernel(
    field_ref, cot_hbm, back_ref, inv_ref, dpre_ref, out_ref, cot_ref, sems
):
    rows, columns = field_ref.shape[1:]
    tall = SLABS * rows
    halves = [pl.ds(h * SLABS, SLABS) for h in range(2)]
    loads = [load(cot_hbm.at[at], cot_ref.at[at], sems.at[h]) for h, at in enumerate(halves)]
    cuts = [slice(y, y + TILE) for y in range(0, columns, TILE)]
    for h in range(2):
        at = slice(h * SLABS, (h + 1) * SLABS)
        back = unpack(back_ref, h)
        total = jnp.zeros((tall, out_ref.shape[2] // 2), F32)
        branch = dot(back, inv_ref[:, cuts[0]])
        loads[h].wait()
        held = None
        for m, cut in enumerate(cuts):
            following = dot(back, inv_ref[:, cuts[m + 1]]) if m + 1 < len(cuts) else None
            pre = flat(field_ref[at, :, cut]).astype(F32) + branch
            dpre = (flat(cot_ref[at, :, cut]) * slope(pre)).astype(BF16)
            if held is not None:
                total = total + dot_t(held, inv_ref[:, cuts[m - 1]])
            dpre_ref[at, :, cut] = dpre.reshape(SLABS, rows, TILE)
            held, branch = dpre, following
        total = total + dot_t(held, inv_ref[:, cuts[-1]])
        pack(total, out_ref, h)


def row_out_kernel(
    dpre_hbm, back_ref, table_ref, out_hbm, dpre_ref, out_ref, sems, sent_sems
):
    chunks = dpre_ref.shape[0] // CHUNK
    rows, columns = dpre_ref.shape[1:]
    per_half = SLABS // CHUNK
    loads = [
        load(dpre_hbm.at[chunk(i)], dpre_ref.at[chunk(i)], sems.at[i]) for i in range(chunks)
    ]
    stores = []
    for h in range(2):
        back = unpack(back_ref, h)
        for n in range(per_half):
            i = h * per_half + n
            loads[i].wait()
            left = back[n * CHUNK * rows : (n + 1) * CHUNK * rows]
            at = slice(i * CHUNK, (i + 1) * CHUNK)
            for start in range(0, columns, TILE):
                cut = slice(start, start + TILE)
                value = flat(dpre_ref[at, :, cut]).astype(F32) + dot(left, table_ref[:, cut])
                out_ref[at, :, cut] = value.astype(BF16).reshape(CHUNK, rows, TILE)
            stores.append(load(out_ref.at[chunk(i)], out_hbm.at[chunk(i)], sent_sems.at[i]))
    for copy in stores:
        copy.wait()


def stack_parts(values):
    return jnp.concatenate(
        [
            jnp.concatenate(
                [values[:, (2 * h + p) * LANES : (2 * h + p + 1) * LANES] for h in range(2)], axis=1
            )
            for p in range(2)
        ],
        axis=0,
    )


def lay_parts(result, out_ref):
    rows = out_ref.shape[0]
    for h in range(2):
        for p in range(2):
            at = (2 * h + p) * LANES
            out_ref[:, at : at + LANES] = result[
                p * rows : (p + 1) * rows, h * LANES : (h + 1) * LANES
            ]


def column_kernel(table_ref, in_ref, *early_and_out):
    out_ref = early_and_out[-1]
    lay_parts(dot(table_ref[...], stack_parts(in_ref[...])).astype(BF16), out_ref)


def weight_kernel(in_ref, *early_and_out):
    out_ref = early_and_out[-1]
    modes, channels = in_ref.shape[0], in_ref.shape[2]
    zero = jnp.zeros((2 * channels, 2 * channels), F32)
    for j in range(modes):
        for pair in range(GROUP // 2):
            blocks = []
            for i in range(2):
                w = in_ref[j, 2 * pair + i].astype(F32)
                turned = jnp.concatenate([-w[:, channels:], w[:, :channels]], axis=1)
                block = jnp.concatenate([w, turned], axis=0)
                blocks.append(
                    jnp.concatenate([block, zero] if i == 0 else [zero, block], axis=1)
                )
            out_ref[pair, :, j * LANES : (j + 1) * LANES] = jnp.concatenate(blocks, axis=0).astype(
                BF16
            )


def own_row(shape, axis):
    return lax.broadcasted_iota(jnp.int32, shape, axis) % GROUP


def mix_kernel(transposed, in_ref, weight_ref, order_ref, order_t_ref, out_ref):
    values = dot(in_ref[...], order_ref[...]).astype(BF16)
    rows = values.shape[0]
    own = own_row((rows, LANES), 0)
    pieces = []
    for pair in range(GROUP // 2):
        left = values[:, pair * LANES : (pair + 1) * LANES]
        total = jnp.zeros((rows, LANES), F32)
        for j in range(GROUP):
            weight = weight_ref[pair, :, j * LANES : (j + 1) * LANES]
            term = dot_t(left, weight) if transposed else dot(left, weight)
            total = jnp.where(own == j, term, total)
        pieces.append(total.astype(BF16))
    mixed = jnp.concatenate(pieces, axis=1)
    out_ref[...] = dot(mixed, order_t_ref[...]).astype(BF16)


def grad_kernel(spec_ref, dmixed_ref, order_ref, early_ref, out_ref):
    spec = dot(spec_ref[...], order_ref[...])
    dmixed = dot(dmixed_ref[...], order_ref[...]).astype(BF16)
    rows = spec.shape[0]
    channels = out_ref.shape[2]
    own = own_row((LANES, rows), 1)
    for pair in range(GROUP // 2):
        left = spec[:, pair * LANES : (pair + 1) * LANES].T
        right = dmixed[:, pair * LANES : (pair + 1) * LANES]
        for j in range(GROUP):
            outer = dot(jnp.where(own == j, left, 0.0).astype(BF16), right)
            for i in range(2):
                at = 2 * channels * i
                re = outer[at : at + channels, at : at + 2 * channels]
                im = outer[at + channels : at + 2 * channels, at : at + 2 * channels]
                turned = jnp.concatenate([im[:, channels:], -im[:, :channels]], axis=1)
                out_ref[j, 2 * pair + i] = re + turned


def shaped(shape, dtype=BF16):
    return jax.ShapeDtypeStruct(shape, dtype)


def call(kernel, out, name, vmem=16, **kw):
    return pl.pallas_call(
        kernel,
        out_shape=out,
        name=name,
        compiler_params=pltpu.CompilerParams(vmem_limit_bytes=vmem * MIB),
        **kw,
    )


HBM = pl.BlockSpec(memory_space=pltpu.HBM)
WHOLE = pl.BlockSpec(memory_space=pltpu.VMEM)


def buffers(*shapes):
    return [pltpu.VMEM(shape, BF16) for shape in shapes]


def sems(count):
    return pltpu.SemaphoreType.DMA((count,))


def across(values, axis):
    return lax.all_to_all(values, axis, split_axis=0, concat_axis=0, tiled=True)


def local(field_in, cotangent, spectral_weight):
    channels, rows_here, columns = field_in.shape[1:]
    pencils = lax.axis_size("pencil")
    modes_y = spectral_weight.shape[1] * pencils
    modes_x = spectral_weight.shape[0] * lax.axis_size("dp")
    height = rows_here * pencils
    wide = 4 * LANES
    chunks = channels // CHUNK
    row_fwd_t, row_inv = row_tables(columns, modes_y)
    col_fwd, col_inv = column_tables(height, modes_x)
    order = mode_order(channels)
    field = field_in[0]
    cot = cotangent[0]
    field_shape = field.shape
    sent_shape = (SLABS, rows_here, wide)
    tall = (columns, 2 * modes_y)
    inv_table, row_table = jnp.asarray(row_inv), jnp.asarray(row_fwd_t)

    def turned(table):
        return jnp.asarray(np.ascontiguousarray(table.T))

    def column(table, values, name, *early):
        return call(column_kernel, shaped((table.shape[0] // 2, wide)), name)(
            table, values, *early
        )

    order_in, order_out = jnp.asarray(order), turned(order)
    fwd_table, col_table = jnp.asarray(col_fwd), jnp.asarray(col_inv)
    weights = call(
        weight_kernel, shaped((GROUP // 2, LANES, GROUP * LANES)), "weight_blocks"
    )(
        spectral_weight.reshape(GROUP, GROUP, channels, 2 * channels),
        order_in, order_out, col_table,
    )

    def mix(values, transposed, name):
        kernel = functools.partial(mix_kernel, transposed)
        mixed = call(kernel, shaped((modes_x, wide)), name)(values, weights, order_in, order_out)
        return across(mixed, "dp")

    sent = call(
        row_in_kernel, shaped(sent_shape), "row_in", 60,
        in_specs=[HBM] * 2, out_specs=WHOLE,
        scratch_shapes=buffers(field_shape, tall) + [sems(3)],
    )(field, turned(row_fwd_t))
    arrived = across(sent, "pencil").reshape(height, wide)
    modes = column(fwd_table, arrived, "column_in", weights)
    spectrum = across(modes, "dp")
    mixed = mix(spectrum, False, "mix")
    back = across(column(col_table, mixed, "column_out", inv_table), "pencil")
    dpre, sent = call(
        middle_kernel, [shaped(field_shape), shaped(sent_shape)], "middle", 40,
        in_specs=[WHOLE, HBM, WHOLE, WHOLE], out_specs=[WHOLE] * 2,
        scratch_shapes=buffers(field_shape) + [sems(2)],
    )(field, cot, back.reshape(sent_shape), inv_table)
    arrived = across(sent, "pencil").reshape(height, wide)
    dmixed = across(column(turned(col_inv), arrived, "column_in_t"), "dp")
    dspectrum = mix(dmixed, True, "mix_t")
    grad_weight = call(
        grad_kernel, shaped((GROUP, GROUP, channels, 2 * channels), F32), "weight_grad",
    )(spectrum, dmixed, order_in, row_table).reshape(spectral_weight.shape)
    sent = call(
        column_kernel, shaped((height, wide)), "column_out_t",
        in_specs=[WHOLE, WHOLE, HBM], out_specs=WHOLE,
    )(turned(col_fwd), dspectrum, grad_weight)
    back = across(sent, "pencil").reshape(sent_shape)
    grad_input = call(
        row_out_kernel, shaped(field_shape), "row_out", 52,
        in_specs=[HBM, WHOLE, WHOLE], out_specs=HBM,
        scratch_shapes=buffers(field_shape, field_shape) + [sems(chunks)] * 2,
    )(dpre, back, row_table)
    return (grad_input[None], grad_weight)


def solution(mesh):
    return jax.shard_map(
        local,
        mesh=mesh,
        in_specs=(
            P("dp", None, "pencil", None),
            P("dp", None, "pencil", None),
            P("dp", "pencil", None),
        ),
        out_specs=(P("dp", None, "pencil", None), P("dp", "pencil", None)),
        check_vma=False,
    )
```
